32 devices in a mesh: rep: 2 (over x), feat: 16 (over z, y, core).
Axes of the slice: x: 2, y: 2, z: 4, core: 2. Of those that a mesh axis runs over, the one named last changes fastest.
Arguments:
- tokens: bfloat16 [3, 32, 16384], P(None, ('rep', 'feat')), parts along dimension 1, may hold values from -6 to 6
- query_weight: bfloat16 [16384, 16384], P(None, 'feat'), may hold values from -0.046875 to 0.046875
- adapter_down_weight: bfloat16 [64, 16384, 128], P(None, 'feat'), may hold values from -0.046875 to 0.046875
- adapter_up_weight: bfloat16 [64, 128, 16384], P(None, None, 'feat'), may hold values from -0.5 to 0.5
- adapter_index_table: int32 [3, 32], P(None, 'rep'), parts along dimension 1, may hold values from 0 to 63
- adapter_rank_sizes: int32 [64], replicated, may hold values from 16 to 128, as said below
Outputs:
- queries: bfloat16 [3, 32, 16384], P(None, ('rep', 'feat')), parts along dimension 1
The draws below stay inside these ranges and needn't reach their ends.
There are 2 independent parts, one for each index of `rep`. The reference program is written for one: setup_inputs(seed, part) draws one part's arguments, and reference() takes and returns one part's arrays. A program takes and returns all parts, laid end to end along the dimension named above; an argument that names none is the same for every part. Nothing has to cross between parts.
Inputs may be any that keep to these rules, and one draw needn't show every extreme that they name: `adapter_rank_sizes`: a multiple of 16.
All inputs are finite; a program needn't handle non-finite values.
Results may differ from the reference program's by a relative error of at most 0.0027.
Values may be sent and summed in bfloat16 or wider, within the bound.
No kernel may reach another device: no remote copies, remote signals or barrier semaphores. Data moves between devices by JAX's collectives and lax.ppermute only.
A program may use at most 192 MiB of HBM per device.

```python
import jax
import jax.numpy as jnp
from jax import lax

MODEL_WIDTH = 16384
RANK_BLOCK = 128
ADAPTER_COUNT = 64
STEPS = 3
BATCH = 16


def draw_adapter_rank_sizes(key, part):
    key = jax.random.fold_in(key, 7)
    first, second = jax.random.split(key)
    units = jax.random.randint(first, (ADAPTER_COUNT,), 1, 9)
    order = jax.random.permutation(second, ADAPTER_COUNT)
    units = units.at[order[0]].set(1).at[order[1]].set(8)
    return (units * (RANK_BLOCK // 8)).astype(jnp.int32)


def set_ends(result, own_key, smallest, high):
    spot = [jax.random.randint(jax.random.fold_in(own_key, axis), (), 0, length) for axis, length in enumerate(result.shape)]
    widest = result.shape.index(max(result.shape))
    beside = spot[:widest] + [(spot[widest] + 1) % result.shape[widest]] + spot[widest + 1:]
    return result.at[tuple(spot)].set(smallest).at[tuple(beside)].set(high)


def block_scale(rng, extent, cuts, least, high):
    level, own = 1.0, jax.random.fold_in(rng, 6)
    for position, blocks in cuts:
        heights = jnp.exp(jax.random.uniform(jax.random.fold_in(own, position), (blocks,), jnp.float32, least / len(cuts), high / len(cuts)))
        level = level * jnp.repeat(heights, extent[position] // blocks).reshape([-1 if axis == position else 1 for axis in range(len(extent))])
    return level


def bell_draw(stream_key, extent, width, most, pieces=(), dtype=jnp.bfloat16):
    result = width * jax.random.normal(stream_key, extent, jnp.float32)
    if pieces:
        result = result * block_scale(stream_key, extent, pieces, -0.22, 0.18)
    return jnp.clip(result, -most, most).astype(dtype)


def setup_inputs(seed: int = 0, part: int = 0) -> dict:
    key_list = jax.random.split(jax.random.key(seed), 7)
    part_splits = jax.random.split(jax.random.fold_in(key_list[6], part), 7)
    tokens = bell_draw(part_splits[0], (STEPS, BATCH, MODEL_WIDTH), 1.0, 6.0, ((1, 16),))
    query_weight = bell_draw(key_list[1], (MODEL_WIDTH, MODEL_WIDTH), MODEL_WIDTH ** -0.5, 0.046875, ((1, 16),))
    adapter_down_weight = bell_draw(key_list[2], (ADAPTER_COUNT, MODEL_WIDTH, RANK_BLOCK), MODEL_WIDTH ** -0.5, 0.046875, ((1, 16),))
    adapter_up_weight = bell_draw(key_list[3], (ADAPTER_COUNT, RANK_BLOCK, MODEL_WIDTH), RANK_BLOCK ** -0.5, 0.5, ((2, 16),))
    adapter_index_table = set_ends(jax.random.randint(part_splits[4], (STEPS, BATCH), 0, ADAPTER_COUNT), jax.random.fold_in(part_splits[4], 1), 0, ADAPTER_COUNT - 1).astype(jnp.int32)
    adapter_rank_sizes = draw_adapter_rank_sizes(jax.random.fold_in(key_list[6], 71), part)
    return {"tokens": tokens, "query_weight": query_weight, "adapter_down_weight": adapter_down_weight, "adapter_up_weight": adapter_up_weight, "adapter_index_table": adapter_index_table, "adapter_rank_sizes": adapter_rank_sizes}


def reference(tokens, query_weight, adapter_down_weight, adapter_up_weight, adapter_index_table, adapter_rank_sizes):
    results = []
    for step in range(STEPS):
        rows = tokens[step]
        adapter_indices = adapter_index_table[step]
        base = jnp.dot(rows, query_weight, preferred_element_type=jnp.float32)

        def shrink(item):
            row, adapter_index = item
            down_matrix = lax.dynamic_index_in_dim(adapter_down_weight, adapter_index, 0, keepdims=False)
            return jnp.dot(row[None, :], down_matrix, preferred_element_type=jnp.float32)[0]

        hidden = lax.map(shrink, (rows, adapter_indices))
        rank_rows = adapter_rank_sizes[adapter_indices]
        keep = jnp.arange(RANK_BLOCK)[None, :] < rank_rows[:, None]
        factor = 0.25 * RANK_BLOCK / rank_rows.astype(jnp.float32)
        reduced_state = jnp.where(keep, hidden * factor[:, None], jnp.float32(0.0)).astype(jnp.bfloat16)

        def expand(item):
            low, adapter_index = item
            up_matrix = lax.dynamic_index_in_dim(adapter_up_weight, adapter_index, 0, keepdims=False)
            return jnp.dot(low[None, :], up_matrix, preferred_element_type=jnp.float32)[0]

        adapter_update = lax.map(expand, (reduced_state, adapter_indices))
        results.append((base + adapter_update).astype(jnp.bfloat16))
    return jnp.stack(results, 0)
```

```python
import functools

import jax
import jax.numpy as jnp
from jax import lax
from jax.experimental import pallas as pl
from jax.experimental.pallas import tpu as pltpu
from jax.sharding import PartitionSpec as P

VMEM, SMEM, ANY = pltpu.VMEM, pltpu.SMEM, pl.ANY
GROUP = 4
LANES = 128


def start_slices(table_ref, weight_ref, held, sems, seen, listed):
    steps, owners = table_ref.shape
    width = 128

    def clear(i, carry):
        seen[i] = jnp.int32(0)
        return carry

    def unlist(i, carry):
        listed[i] = jnp.int32(-1)
        return carry

    lax.fori_loop(0, weight_ref.shape[0], clear, 0)
    lax.fori_loop(0, held.shape[0], unlist, 0)

    def one(b, count):
        adapter = table_ref[b % steps, b // steps]
        new = seen[adapter] == 0

        @pl.when(new)
        def _():
            seen[adapter] = jnp.int32(1)
            listed[count] = adapter
            pltpu.make_async_copy(weight_ref.at[adapter], held.at[count], sems.at[count]).start()

        return count + new.astype(jnp.int32)

    return lax.fori_loop(0, steps * owners, one, jnp.int32(0))


def wait_group(group, count, listed, weight_ref, held, sems):
    for i in range(GROUP):
        slot = group * GROUP + i

        @pl.when(slot < count)
        def _():
            pltpu.make_async_copy(weight_ref.at[0], held.at[slot], sems.at[slot]).wait()


def down_kernel(order, me_ref, table_ref, adapter_rows_ref, *refs):
    parts = refs[: len(order)]
    weight_ref, lhs_ref, partial_ref, wide, held, seen, listed, sems = refs[len(order) :]
    count = start_slices(table_ref, weight_ref, held, sems, seen, listed)
    chunks, rows, depth = lhs_ref.shape
    block = rows // chunks * chunks
    me = me_ref[0]
    for part, owners in zip(parts, order, strict=True):
        for place, distance in enumerate(owners):
            owner = jnp.bitwise_xor(me, distance)
            at = pl.ds(pl.multiple_of(owner * block, block), block)
            for tile in range(depth // LANES):
                piece = part[place * block : (place + 1) * block, tile * LANES : (tile + 1) * LANES]
                wide[tile, at, :] = piece.astype(jnp.float32)
    for chunk in range(chunks):
        for tile in range(depth // LANES):
            piece = wide[tile, pl.ds(chunk, rows, stride=chunks), :]
            lhs_ref[chunk, :, tile * LANES : (tile + 1) * LANES] = piece.astype(jnp.bfloat16)
    mine = lhs_ref[me]
    adapter_rows = adapter_rows_ref[...]

    def one(group, total):
        wait_group(group, count, listed, weight_ref, held, sems)
        for pair in range(0, GROUP, 2):
            slot = group * GROUP + pair
            both = jnp.concatenate([held[slot], held[slot + 1]], axis=1)
            product = jnp.dot(mine, both, preferred_element_type=jnp.float32)
            half = product.shape[1] // 2
            total = jnp.where(adapter_rows == listed[slot], product[:, :half], total)
            total = jnp.where(adapter_rows == listed[slot + 1], product[:, half:], total)
        return total

    zeros = jnp.zeros(partial_ref.shape, jnp.float32)
    partial_ref[...] = lax.fori_loop(0, (count + GROUP - 1) // GROUP, one, zeros)


def base_kernel(lhs_ref, weight_ref, out_ref, held, sems):
    chunks, rows, depth = lhs_ref.shape
    copies = []
    for chunk in range(chunks):
        copy = pltpu.make_async_copy(weight_ref.at[pl.ds(chunk * depth, depth)], held.at[chunk], sems.at[chunk])
        copy.start()
        copies.append(copy)
    total = jnp.zeros(out_ref.shape, jnp.float32)
    for chunk in range(chunks):
        copies[chunk].wait()
        total += jnp.dot(lhs_ref[chunk], held[chunk], preferred_element_type=jnp.float32)
    out_ref[...] = total


def up_kernel(table_ref, adapter_rows_ref, rank_rows_ref, hidden_ref, base_ref, weight_ref, out_ref, held, seen, listed, sems):
    count = start_slices(table_ref, weight_ref, held, sems, seen, listed)
    width = hidden_ref.shape[1]
    rank_rows = rank_rows_ref[...]
    keep = lax.broadcasted_iota(jnp.int32, rank_rows.shape, 1) < rank_rows
    factor = 0.25 * width / rank_rows.astype(jnp.float32)
    lowrank = jnp.where(keep, hidden_ref[...] * factor, jnp.float32(0.0))
    adapter_rows = adapter_rows_ref[...]

    def one(group, total):
        wait_group(group, count, listed, weight_ref, held, sems)
        for i in range(GROUP):
            slot = group * GROUP + i
            own = jnp.where(adapter_rows == listed[slot], lowrank, jnp.float32(0.0)).astype(jnp.bfloat16)
            matrix = held[slot]
            product = jnp.dot(own, matrix, preferred_element_type=jnp.float32)
            hit = adapter_rows[:, :1] == listed[slot]
            total = total + jnp.where(hit, product, jnp.float32(0.0))
        return total

    total = lax.fori_loop(0, (count + GROUP - 1) // GROUP, one, base_ref[...])
    total = total.astype(jnp.bfloat16)
    steps = out_ref.shape[1]
    for owner in range(out_ref.shape[0]):
        out_ref[owner] = total[owner * steps : (owner + 1) * steps, :]


def exchange(value, distance, ranks):
    return lax.ppermute(value, "feat", [(i, i ^ distance) for i in range(ranks)])


def fast(tokens, query_weight, adapter_down_weight, adapter_up_weight, adapter_index_table, adapter_rank_sizes):
    steps, _, features = tokens.shape
    ranks = adapter_index_table.shape[1]
    columns = query_weight.shape[1]
    adapters, depth, width = adapter_down_weight.shape
    rows = steps * ranks
    swap = functools.partial(exchange, ranks=ranks)
    spec = lambda space: pl.BlockSpec(memory_space=space)

    adapter_rows = jnp.broadcast_to(adapter_index_table.T.reshape(rows, 1), (rows, width))
    matches = adapter_rows[:, :1] == jnp.arange(adapters)[None, :]
    rank_rows = jnp.sum(jnp.where(matches, adapter_rank_sizes[None, :], 0), axis=1, keepdims=True)
    rank_rows = jnp.broadcast_to(rank_rows, (rows, width))
    me = lax.axis_index("feat").astype(jnp.int32).reshape(1)

    own = tokens.reshape(steps * ranks, features // ranks)
    near = jnp.concatenate([own, swap(own, 4), swap(own, 8), swap(own, 12)], axis=0)
    far = swap(near, 2)
    parts = (near, far, swap(near, 1), swap(far, 1))
    order = tuple(tuple(first ^ z for z in (0, 4, 8, 12)) for first in (0, 2, 1, 3))

    lhs, partial = pl.pallas_call(
        functools.partial(down_kernel, order),
        out_shape=(
            jax.ShapeDtypeStruct((ranks, rows, features // ranks), jnp.bfloat16),
            jax.ShapeDtypeStruct((rows, width), jnp.float32),
        ),
        in_specs=[spec(SMEM), spec(SMEM), spec(VMEM)] + [spec(VMEM)] * len(parts) + [spec(ANY)],
        out_specs=(spec(VMEM), spec(VMEM)),
        scratch_shapes=[
            VMEM((depth // LANES, rows * ranks, LANES), jnp.float32),
            VMEM((rows, depth, width), jnp.bfloat16),
            SMEM((adapters,), jnp.int32),
            SMEM((rows,), jnp.int32),
            pltpu.SemaphoreType.DMA((rows,)),
        ],
        compiler_params=pltpu.CompilerParams(vmem_limit_bytes=48 << 20),
        cost_estimate=pl.CostEstimate(flops=2 * rows * depth * width, bytes_accessed=12 << 20, transcendentals=0),
    )(me, adapter_index_table, adapter_rows, *parts, adapter_down_weight)

    base = pl.pallas_call(
        base_kernel,
        out_shape=jax.ShapeDtypeStruct((rows, columns), jnp.float32),
        in_specs=[spec(VMEM), spec(ANY)],
        out_specs=spec(VMEM),
        scratch_shapes=[
            VMEM((ranks, features // ranks, columns), jnp.bfloat16),
            pltpu.SemaphoreType.DMA((ranks,)),
        ],
        compiler_params=pltpu.CompilerParams(vmem_limit_bytes=48 << 20),
        cost_estimate=pl.CostEstimate(flops=2 * rows * features * columns, bytes_accessed=34 << 20, transcendentals=0),
    )(lhs, query_weight)

    hidden = partial + swap(partial, 1)
    hidden = hidden + swap(hidden, 2) + swap(hidden, 4) + swap(hidden, 6)
    hidden = hidden + swap(hidden, 8)

    out = pl.pallas_call(
        up_kernel,
        out_shape=jax.ShapeDtypeStruct((ranks, steps, columns), jnp.bfloat16),
        in_specs=[spec(SMEM)] + [spec(VMEM)] * 4 + [spec(ANY)],
        out_specs=spec(VMEM),
        scratch_shapes=[
            VMEM((rows, width, columns), jnp.bfloat16),
            SMEM((adapters,), jnp.int32),
            SMEM((rows,), jnp.int32),
            pltpu.SemaphoreType.DMA((rows,)),
        ],
        compiler_params=pltpu.CompilerParams(vmem_limit_bytes=48 << 20),
        cost_estimate=pl.CostEstimate(flops=2 * rows * width * columns, bytes_accessed=12 << 20, transcendentals=0),
    )(adapter_index_table, adapter_rows, rank_rows, hidden, base, adapter_up_weight)

    gathered = lax.all_to_all(out, "feat", split_axis=0, concat_axis=0, tiled=True)
    return gathered.transpose(1, 0, 2).reshape(steps, 1, features)


def plain(tokens, query_weight, adapter_down_weight, adapter_up_weight, adapter_index_table, adapter_rank_sizes):
    width = query_weight.shape[1]
    rank_width = adapter_down_weight.shape[2]
    depth = adapter_down_weight.shape[1]
    whole = lax.all_gather(tokens, "feat", axis=1, tiled=True)
    piece = lax.dynamic_slice_in_dim(whole, lax.axis_index("feat") * depth, depth, 2)
    matrices = adapter_down_weight[adapter_index_table]
    partial = jnp.einsum("xun,xune->xue", piece, matrices, preferred_element_type=jnp.float32)
    hidden = lax.psum(partial, "feat")
    rank_rows = adapter_rank_sizes[adapter_index_table]
    keep = jnp.arange(rank_width)[None, None, :] < rank_rows[:, :, None]
    factor = 0.25 * rank_width / rank_rows.astype(jnp.float32)
    lowrank = jnp.where(keep, hidden * factor[:, :, None], jnp.float32(0.0)).astype(jnp.bfloat16)
    matrices = adapter_up_weight[adapter_index_table]
    update = jnp.einsum("jma,jmap->jmp", lowrank, matrices, preferred_element_type=jnp.float32)
    base = jnp.einsum("sbd,dc->sbc", whole, query_weight, preferred_element_type=jnp.float32)
    out = (base + update).astype(jnp.bfloat16)
    return lax.all_to_all(out, "feat", split_axis=1, concat_axis=2, tiled=True)


def on_device(tokens, query_weight, *rest):
    ranks = rest[2].shape[1]
    fits = ranks == 16 and query_weight.shape[1] % 256 == 0
    return (fast if fits else plain)(tokens, query_weight, *rest)


def solution(mesh):
    in_specs = (
        P(None, ("rep", "feat"), None),
        P(None, "feat"),
        P(None, "feat", None),
        P(None, None, "feat"),
        P(None, "rep"),
        P(),
    )
    out_specs = P(None, ("rep", "feat"), None)
    return jax.shard_map(
        on_device, mesh=mesh, in_specs=in_specs, out_specs=out_specs, check_vma=False
    )
```

```python
import functools

import jax
import jax.numpy as jnp
from jax import lax
from jax.experimental import pallas as pl
from jax.experimental.pallas import tpu as pltpu
from jax.sharding import PartitionSpec as P

VMEM, SMEM, ANY = pltpu.VMEM, pltpu.SMEM, pl.ANY
GROUP = 4
LANES = 128


def list_adapters(table_ref, seen, listed):
    steps, owners = table_ref.shape
    rows = steps * owners

    def clear(i, carry):
        seen[i] = jnp.int32(0)
        return carry

    def unlist(i, carry):
        listed[i] = jnp.int32(-1)
        return carry

    lax.fori_loop(0, seen.shape[0], clear, 0)
    lax.fori_loop(0, rows, unlist, 0)
    count = jnp.int32(0)
    for b in range(rows):
        adapter = table_ref[b % steps, b // steps]
        new = seen[adapter] == 0

        @pl.when(new)
        def _():
            seen[adapter] = jnp.int32(1)
            listed[count] = adapter

        count = count + new.astype(jnp.int32)
    listed[rows] = count


def padded(count):
    return (count + GROUP - 1) // GROUP * GROUP


def start_slices(listed, weight_ref, held, sem):
    def one(slot, carry):
        adapter = jnp.maximum(listed[slot], 0)
        pltpu.make_async_copy(weight_ref.at[adapter], held.at[slot], sem).start()
        return carry

    lax.fori_loop(0, padded(listed[held.shape[0]]), one, 0)


def wait_slices(listed, weight_ref, held, sem):
    def one(slot, carry):
        pltpu.make_async_copy(weight_ref.at[0], held.at[slot], sem).wait()
        return carry

    lax.fori_loop(0, padded(listed[held.shape[0]]), one, 0)


def fetch_kernel(first, weight_ref, *refs):
    held, sem = refs[-2:]
    copy = pltpu.make_async_copy(weight_ref.at[pl.ds(first, held.shape[0])], held, sem)
    copy.start()
    copy.wait()


def fetch_both_kernel(first, table_ref, weight_ref, slices_ref, held, slices, listed, seen, sem, slice_sem):
    copy = pltpu.make_async_copy(weight_ref.at[pl.ds(first, held.shape[0])], held, sem)
    copy.start()
    list_adapters(table_ref, seen, listed)
    start_slices(listed, slices_ref, slices, slice_sem)
    wait_slices(listed, slices_ref, slices, slice_sem)
    copy.wait()


def down_kernel(listed, place_ref, adapter_rows_ref, *refs):
    *parts, slices, out_ref = refs
    rows, width = out_ref.shape
    place = place_ref[...][:, :1]
    mine = jnp.zeros((rows, slices.shape[1]), jnp.float32)
    first = 0
    for part in parts:
        chosen = lax.broadcasted_iota(jnp.int32, (rows, part.shape[0]), 1) + first == place
        chosen = jnp.where(chosen, jnp.float32(1.0), jnp.float32(0.0)).astype(jnp.bfloat16)
        mine += jnp.dot(chosen, part[...], preferred_element_type=jnp.float32)
        first += part.shape[0]
    mine = mine.astype(jnp.bfloat16)
    adapter_rows = adapter_rows_ref[...]

    def one(group, total):
        for pair in range(0, GROUP, 2):
            slot = group * GROUP + pair
            both = jnp.concatenate([slices[slot], slices[slot + 1]], axis=1)
            product = jnp.dot(mine, both, preferred_element_type=jnp.float32)
            total = jnp.where(adapter_rows == listed[slot], product[:, :width], total)
            total = jnp.where(adapter_rows == listed[slot + 1], product[:, width:], total)
        return total

    zeros = jnp.zeros((rows, width), jnp.float32)
    out_ref[...] = lax.fori_loop(0, padded(listed[rows]) // GROUP, one, zeros)


def first_base_kernel(order, me_ref, listed, *refs):
    parts = refs[: len(order)]
    weight, slices_ref, lhs_ref, out_ref, slices, wide, slice_sem = refs[len(order) :]
    start_slices(listed, slices_ref, slices, slice_sem)
    chunks, rows, depth = lhs_ref.shape
    block = rows // chunks * chunks
    me = me_ref[0]
    for part, owners in zip(parts, order, strict=True):
        for place, distance in enumerate(owners):
            owner = jnp.bitwise_xor(me, distance)
            at = pl.ds(pl.multiple_of(owner * block, block), block)
            for tile in range(depth // LANES):
                piece = part[place * block : (place + 1) * block, tile * LANES : (tile + 1) * LANES]
                wide[tile, at, :] = piece.astype(jnp.float32)
    for chunk in range(chunks):
        for tile in range(depth // LANES):
            piece = wide[tile, pl.ds(chunk, rows, stride=chunks), :]
            lhs_ref[chunk, :, tile * LANES : (tile + 1) * LANES] = piece.astype(jnp.bfloat16)
    total = jnp.zeros(out_ref.shape, jnp.float32)
    for chunk in range(weight.shape[0] // depth):
        matrix = weight[chunk * depth : (chunk + 1) * depth, :]
        total += jnp.dot(lhs_ref[chunk], matrix, preferred_element_type=jnp.float32)
    out_ref[...] = total
    wait_slices(listed, slices_ref, slices, slice_sem)


def rest_base_kernel(lhs_ref, base_ref, weight, rest_ref, out_ref, rest, sems):
    chunks, rows, depth = lhs_ref.shape
    start = rest_ref.shape[0] - rest.shape[0] * depth
    copies = []
    for chunk in range(rest.shape[0]):
        there = rest_ref.at[pl.ds(start + chunk * depth, depth)]
        copies.append(pltpu.make_async_copy(there, rest.at[chunk], sems.at[chunk]))
        copies[chunk].start()
    total = base_ref[...]
    here = weight.shape[0] // depth
    first = chunks - here - len(copies)
    for chunk in range(here):
        matrix = weight[chunk * depth : (chunk + 1) * depth, :]
        total += jnp.dot(lhs_ref[first + chunk], matrix, preferred_element_type=jnp.float32)
    for chunk in range(len(copies)):
        copies[chunk].wait()
        total += jnp.dot(lhs_ref[first + here + chunk], rest[chunk], preferred_element_type=jnp.float32)
    out_ref[...] = total


def up_kernel(listed, adapter_rows_ref, rank_rows_ref, hidden_ref, base_ref, slices, out_ref):
    rows, width = hidden_ref.shape
    rank_rows = rank_rows_ref[...]
    keep = lax.broadcasted_iota(jnp.int32, rank_rows.shape, 1) < rank_rows
    factor = 0.25 * width / rank_rows.astype(jnp.float32)
    lowrank = jnp.where(keep, hidden_ref[...] * factor, jnp.float32(0.0))
    adapter_rows = adapter_rows_ref[...]

    def one(group, total):
        slot = group * GROUP
        own = [jnp.where(adapter_rows == listed[slot + i], lowrank, jnp.float32(0.0)) for i in range(GROUP)]
        own = jnp.concatenate(own, axis=1).astype(jnp.bfloat16)
        matrix = jnp.concatenate([slices[slot + i] for i in range(GROUP)], axis=0)
        return total + jnp.dot(own, matrix, preferred_element_type=jnp.float32)

    total = lax.fori_loop(0, padded(listed[rows]) // GROUP, one, base_ref[...])
    total = total.astype(jnp.bfloat16)
    steps = out_ref.shape[1]
    for owner in range(out_ref.shape[0]):
        out_ref[owner] = total[owner * steps : (owner + 1) * steps, :]


def exchange(value, distance, ranks):
    return lax.ppermute(value, "feat", [(i, i ^ distance) for i in range(ranks)])


def spec(space, count=1):
    return [pl.BlockSpec(memory_space=space)] * count


def cost(flops, size):
    return pl.CostEstimate(flops=flops, bytes_accessed=size, transcendentals=0)


def held_here(value):
    return pltpu.with_memory_space_constraint(value, VMEM)


def left_there(value):
    return pltpu.with_memory_space_constraint(value, pltpu.HBM)


def fast(tokens, query_weight, adapter_down_weight, adapter_up_weight, adapter_index_table, adapter_rank_sizes):
    steps, _, features = tokens.shape
    ranks = adapter_index_table.shape[1]
    columns = query_weight.shape[1]
    adapters, depth, width = adapter_down_weight.shape
    rows = steps * ranks
    bf16, f32 = jnp.bfloat16, jnp.float32
    swap = functools.partial(exchange, ranks=ranks)
    shape = jax.ShapeDtypeStruct
    params = pltpu.CompilerParams(vmem_limit_bytes=5 << 20)
    flops = 2 * rows * features * columns

    adapter_rows = jnp.broadcast_to(adapter_index_table.T.reshape(rows, 1), (rows, width))
    matches = adapter_rows[:, :1] == jnp.arange(adapters)[None, :]
    rank_rows = jnp.sum(jnp.where(matches, adapter_rank_sizes[None, :], 0), axis=1, keepdims=True)
    rank_rows = jnp.broadcast_to(rank_rows, (rows, width))
    me = lax.axis_index("feat").astype(jnp.int32)
    row = jnp.arange(rows, dtype=jnp.int32)
    distance = (row // steps) ^ me
    number = (distance & 1) * 2 + ((distance >> 1) & 1)
    place = (number * (ranks // 4) + (distance >> 2)) * rows + (row % steps) * ranks + me
    place = jnp.broadcast_to(place[:, None], (rows, width))
    me = me.reshape(1)
    order = tuple(tuple(first ^ z for z in (0, 4, 8, 12)) for first in (0, 2, 1, 3))

    early, late = features // 16 * 7, features // 16 * 4
    weight_early = pl.pallas_call(
        functools.partial(fetch_kernel, 0),
        out_shape=VMEM((early, columns), bf16),
        in_specs=spec(ANY, 5),
        out_specs=spec(VMEM)[0],
        scratch_shapes=[pltpu.SemaphoreType.DMA],
        compiler_params=params,
        cost_estimate=cost(0, early * columns * 2),
    )(left_there(query_weight), me, place, adapter_rows, rank_rows)
    own = tokens.reshape(steps * ranks, features // ranks)
    across = (swap(own, 4), swap(own, 8), swap(own, 12))
    across, weight_early = lax.optimization_barrier((across, weight_early))
    near = jnp.concatenate([own, *across], axis=0)
    weight_late, down_slices, listed = pl.pallas_call(
        functools.partial(fetch_both_kernel, early),
        out_shape=(
            VMEM((late, columns), bf16),
            VMEM((rows, depth, width), bf16),
            shape((rows + 1,), jnp.int32),
        ),
        in_specs=spec(SMEM) + spec(ANY, 2),
        out_specs=spec(VMEM, 2) + spec(SMEM),
        scratch_shapes=[
            SMEM((adapters,), jnp.int32),
            pltpu.SemaphoreType.DMA,
            pltpu.SemaphoreType.DMA,
        ],
        compiler_params=params,
        cost_estimate=cost(0, late * columns * 2 + rows * depth * width * 2),
    )(adapter_index_table, left_there(query_weight), left_there(adapter_down_weight))
    far = swap(near, 2)
    far, weight_late, down_slices, listed = lax.optimization_barrier((far, weight_late, down_slices, listed))
    parts = (near, far, swap(near, 1), swap(far, 1))

    hidden = pl.pallas_call(
        down_kernel,
        out_shape=shape((rows, width), f32),
        in_specs=spec(SMEM) + spec(VMEM, 2 + len(parts) + 1),
        out_specs=spec(VMEM)[0],
        compiler_params=params,
        cost_estimate=cost(2 * rows * depth * width * rows, 1 << 20),
    )(listed, place, adapter_rows, *parts, held_here(down_slices))

    lhs, base, up_slices = pl.pallas_call(
        functools.partial(first_base_kernel, order),
        out_shape=(
            shape((ranks, rows, features // ranks), bf16),
            shape((rows, columns), f32),
            VMEM((rows, width, columns), bf16),
        ),
        in_specs=spec(SMEM, 2) + spec(VMEM, len(parts) + 1) + spec(ANY),
        out_specs=spec(VMEM, 3),
        scratch_shapes=[
            VMEM((depth // LANES, rows * ranks, LANES), f32),
            pltpu.SemaphoreType.DMA,
        ],
        compiler_params=params,
        cost_estimate=cost(flops // 2, 16 << 20),
    )(me, listed, *parts, held_here(weight_early), left_there(adapter_up_weight))

    hidden = hidden + swap(hidden, 1)
    three = (swap(hidden, 2), swap(hidden, 4), swap(hidden, 6))
    three, lhs, base, up_slices = lax.optimization_barrier((three, lhs, base, up_slices))
    hidden = hidden + three[0] + three[1] + three[2]

    base = pl.pallas_call(
        rest_base_kernel,
        out_shape=shape((rows, columns), f32),
        in_specs=spec(VMEM, 3) + spec(ANY),
        out_specs=spec(VMEM)[0],
        scratch_shapes=[
            VMEM((5, features // ranks, columns), bf16),
            pltpu.SemaphoreType.DMA((5,)),
        ],
        compiler_params=pltpu.CompilerParams(vmem_limit_bytes=15 << 20),
        cost_estimate=cost(flops // 2, 10 << 20),
    )(lhs, base, held_here(weight_late), left_there(query_weight))
    last, base = lax.optimization_barrier((swap(hidden, 8), base))
    hidden = hidden + last

    out = pl.pallas_call(
        up_kernel,
        out_shape=shape((ranks, steps, columns), bf16),
        in_specs=spec(SMEM) + spec(VMEM, 5),
        out_specs=spec(VMEM)[0],
        compiler_params=params,
        cost_estimate=cost(2 * rows * width * columns * rows, 1 << 20),
    )(listed, adapter_rows, rank_rows, hidden, base, held_here(up_slices))

    gathered = lax.all_to_all(out, "feat", split_axis=0, concat_axis=0, tiled=True)
    return gathered.transpose(1, 0, 2).reshape(steps, 1, features)


def plain(tokens, query_weight, adapter_down_weight, adapter_up_weight, adapter_index_table, adapter_rank_sizes):
    width = query_weight.shape[1]
    rank_width = adapter_down_weight.shape[2]
    depth = adapter_down_weight.shape[1]
    whole = lax.all_gather(tokens, "feat", axis=1, tiled=True)
    piece = lax.dynamic_slice_in_dim(whole, lax.axis_index("feat") * depth, depth, 2)
    matrices = adapter_down_weight[adapter_index_table]
    partial = jnp.einsum("xun,xune->xue", piece, matrices, preferred_element_type=jnp.float32)
    hidden = lax.psum(partial, "feat")
    rank_rows = adapter_rank_sizes[adapter_index_table]
    keep = jnp.arange(rank_width)[None, None, :] < rank_rows[:, :, None]
    factor = 0.25 * rank_width / rank_rows.astype(jnp.float32)
    lowrank = jnp.where(keep, hidden * factor[:, :, None], jnp.float32(0.0)).astype(jnp.bfloat16)
    matrices = adapter_up_weight[adapter_index_table]
    update = jnp.einsum("jma,jmap->jmp", lowrank, matrices, preferred_element_type=jnp.float32)
    base = jnp.einsum("sbd,dc->sbc", whole, query_weight, preferred_element_type=jnp.float32)
    out = (base + update).astype(jnp.bfloat16)
    return lax.all_to_all(out, "feat", split_axis=1, concat_axis=2, tiled=True)


def on_device(tokens, query_weight, *rest):
    ranks = rest[2].shape[1]
    fits = ranks == 16 and query_weight.shape[1] % 256 == 0
    return (fast if fits else plain)(tokens, query_weight, *rest)


def solution(mesh):
    in_specs = (
        P(None, ("rep", "feat"), None),
        P(None, "feat"),
        P(None, "feat", None),
        P(None, None, "feat"),
        P(None, "rep"),
        P(),
    )
    out_specs = P(None, ("rep", "feat"), None)
    return jax.shard_map(
        on_device, mesh=mesh, in_specs=in_specs, out_specs=out_specs, check_vma=False
    )
```

```python
import functools

import jax
import jax.numpy as jnp
from jax import lax
from jax.experimental import pallas as pl
from jax.experimental.pallas import tpu as pltpu
from jax.sharding import PartitionSpec as P

VMEM, SMEM, ANY = pltpu.VMEM, pltpu.SMEM, pl.ANY
GROUP = 8
FETCHED = (0, 5, 10, 13)
LANES = 128


def list_adapters(me, table_ref, sizes_ref, seen, listed, adapter_rows, rank_rows, place):
    steps, owners = table_ref.shape
    rows, lanes = adapter_rows.shape
    for i in range(seen.shape[0]):
        seen[i] = jnp.int32(0)
    for i in range(listed.shape[0]):
        listed[i] = jnp.int32(-1)
    count = jnp.int32(0)
    for b in range(rows):
        adapter = table_ref[b % steps, b // steps]
        new = jnp.int32(1) - seen[adapter]
        seen[adapter] = jnp.int32(1)
        listed[count] = adapter
        count = count + new
        distance = jnp.bitwise_xor(me, jnp.int32(b // steps))
        part = (distance & 1) * 2 + ((distance >> 1) & 1)
        across = (distance >> 2) + jnp.where(distance < 4, 0, jnp.where(distance < 8, 2, -1))
        spot = (part * (owners // 4) + across) * rows + (b % steps) * owners + me
        adapter_rows[b : b + 1, :] = jnp.full((1, lanes), adapter, jnp.int32)
        rank_rows[b : b + 1, :] = jnp.full((1, lanes), sizes_ref[adapter], jnp.int32)
        place[b : b + 1, :] = jnp.full((1, lanes), spot, jnp.int32)
    listed[count] = jnp.int32(-1)
    listed[rows + 1] = count


def padded(count):
    return (count + GROUP - 1) // GROUP * GROUP


def start_slices(listed, weight_ref, held, sem):
    def one(slot, carry):
        adapter = jnp.maximum(listed[slot], 0)
        pltpu.make_async_copy(weight_ref.at[adapter], held.at[slot], sem).start()
        return carry

    lax.fori_loop(0, padded(listed[held.shape[0] + 1]), one, 0)


def wait_slices(listed, weight_ref, held, sem):
    def one(slot, carry):
        pltpu.make_async_copy(weight_ref.at[0], held.at[slot], sem).wait()
        return carry

    lax.fori_loop(0, padded(listed[held.shape[0] + 1]), one, 0)


def fetch_rows(first, weight_ref, held, sem):
    return pltpu.make_async_copy(weight_ref.at[pl.ds(first, held.shape[0])], held, sem)


def fetch_and_list_kernel(
    first, me_ref, table_ref, sizes_ref, weight_ref, held, listed, adapter_rows, rank_rows, place, seen, sem
):
    copy = fetch_rows(first, weight_ref, held, sem)
    copy.start()
    list_adapters(me_ref[0], table_ref, sizes_ref, seen, listed, adapter_rows, rank_rows, place)
    copy.wait()


def fetch_both_kernel(first, listed, weight_ref, slices_ref, held, slices, sem, slice_sem):
    start_slices(listed, slices_ref, slices, slice_sem)
    copy = fetch_rows(first, weight_ref, held, sem)
    copy.start()
    wait_slices(listed, slices_ref, slices, slice_sem)
    copy.wait()


def down_kernel(first_row, listed, place_ref, adapter_rows_ref, *refs):
    *parts, slices, weight_ref, out_ref, held, sem = refs
    copy = fetch_rows(first_row, weight_ref, held, sem)
    copy.start()
    rows, width = out_ref.shape
    place = place_ref[...][:, :1]
    mine = jnp.zeros((rows, slices.shape[1]), jnp.float32)
    first = 0
    for part in parts:
        chosen = lax.broadcasted_iota(jnp.int32, (rows, part.shape[0]), 1) + first == place
        chosen = jnp.where(chosen, jnp.float32(1.0), jnp.float32(0.0)).astype(jnp.bfloat16)
        mine += jnp.dot(chosen, part[...], preferred_element_type=jnp.float32)
        first += part.shape[0]
    mine = mine.astype(jnp.bfloat16)
    adapter_rows = adapter_rows_ref[...]

    def one(group, total):
        for pair in range(0, GROUP, 2):
            slot = group * GROUP + pair
            both = jnp.concatenate([slices[slot], slices[slot + 1]], axis=1)
            product = jnp.dot(mine, both, preferred_element_type=jnp.float32)
            total = jnp.where(adapter_rows == listed[slot], product[:, :width], total)
            total = jnp.where(adapter_rows == listed[slot + 1], product[:, width:], total)
        return total

    zeros = jnp.zeros((rows, width), jnp.float32)
    out_ref[...] = lax.fori_loop(0, padded(listed[rows + 1]) // GROUP, one, zeros)
    copy.wait()


def first_base_kernel(order, me_ref, listed, *refs):
    parts = refs[: len(order)]
    weight, slices_ref, lhs_ref, out_ref, slices, wide, slice_sem = refs[len(order) :]
    start_slices(listed, slices_ref, slices, slice_sem)
    rest, rows, depth = lhs_ref.shape
    chunks = rest + weight.shape[0] // depth
    block = rows // chunks * chunks
    me = me_ref[0]
    for part, owners in zip(parts, order, strict=True):
        for place, distance in enumerate(owners):
            owner = jnp.bitwise_xor(me, distance)
            at = pl.ds(pl.multiple_of(owner * block, block), block)
            for tile in range(depth // LANES):
                piece = part[place * block : (place + 1) * block, tile * LANES : (tile + 1) * LANES]
                wide[tile, at, :] = piece.astype(jnp.float32)

    def whole(chunk):
        pieces = [wide[tile, pl.ds(chunk, rows, stride=chunks), :] for tile in range(depth // LANES)]
        return jnp.concatenate(pieces, axis=1).astype(jnp.bfloat16)

    total = jnp.zeros(out_ref.shape, jnp.float32)
    here = weight.shape[0] // depth
    for chunk in range(here):
        matrix = weight[chunk * depth : (chunk + 1) * depth, :]
        total += jnp.dot(whole(chunk), matrix, preferred_element_type=jnp.float32)
        for other in range(here + chunk, chunks, here):
            lhs_ref[other - here] = whole(other)
    out_ref[...] = total
    wait_slices(listed, slices_ref, slices, slice_sem)


def rest_base_kernel(lhs_ref, base_ref, *refs):
    *weights, rest_ref, out_ref, rest, sems = refs
    chunks, rows, depth = lhs_ref.shape
    streamed = rest.shape[0]
    start = rest_ref.shape[0] - streamed * depth
    copies = []
    for i in range(streamed):
        there = rest_ref.at[pl.ds(start + i * depth, depth)]
        copies.append(pltpu.make_async_copy(there, rest.at[i], sems.at[i]))
        copies[i].start()
    total = base_ref[...]
    chunk = 0
    for weight in weights:
        for first in range(0, weight.shape[0], depth):
            matrix = weight[first : first + depth, :]
            total += jnp.dot(lhs_ref[chunk], matrix, preferred_element_type=jnp.float32)
            chunk += 1
    for i in range(streamed):
        copies[i].wait()
        total += jnp.dot(lhs_ref[chunk + i], rest[i], preferred_element_type=jnp.float32)
    out_ref[...] = total


def up_kernel(listed, adapter_rows_ref, rank_rows_ref, hidden_ref, base_ref, slices, out_ref):
    rows, width = hidden_ref.shape
    rank_rows = rank_rows_ref[...]
    keep = lax.broadcasted_iota(jnp.int32, rank_rows.shape, 1) < rank_rows
    factor = 0.25 * width / rank_rows.astype(jnp.float32)
    lowrank = jnp.where(keep, hidden_ref[...] * factor, jnp.float32(0.0))
    adapter_rows = adapter_rows_ref[...]

    def one(group, total):
        slot = group * GROUP
        own = [jnp.where(adapter_rows == listed[slot + i], lowrank, jnp.float32(0.0)) for i in range(GROUP)]
        own = jnp.concatenate(own, axis=1).astype(jnp.bfloat16)
        matrix = jnp.concatenate([slices[slot + i] for i in range(GROUP)], axis=0)
        return total + jnp.dot(own, matrix, preferred_element_type=jnp.float32)

    total = lax.fori_loop(0, padded(listed[rows + 1]) // GROUP, one, base_ref[...])
    total = total.astype(jnp.bfloat16)
    steps = out_ref.shape[1]
    for owner in range(out_ref.shape[0]):
        out_ref[owner] = total[owner * steps : (owner + 1) * steps, :]


def exchange(value, distance, ranks):
    return lax.ppermute(value, "feat", [(i, i ^ distance) for i in range(ranks)])


def spec(space, count=1):
    return [pl.BlockSpec(memory_space=space)] * count


def cost(flops, size):
    return pl.CostEstimate(flops=flops, bytes_accessed=size, transcendentals=0)


def held_here(value):
    return pltpu.with_memory_space_constraint(value, VMEM)


def left_there(value):
    return pltpu.with_memory_space_constraint(value, pltpu.HBM)


def fast(tokens, query_weight, adapter_down_weight, adapter_up_weight, adapter_index_table, adapter_rank_sizes):
    steps, _, features = tokens.shape
    ranks = adapter_index_table.shape[1]
    columns = query_weight.shape[1]
    adapters, depth, width = adapter_down_weight.shape
    rows = steps * ranks
    bf16, f32 = jnp.bfloat16, jnp.float32
    swap = functools.partial(exchange, ranks=ranks)
    shape = jax.ShapeDtypeStruct
    params = pltpu.CompilerParams(vmem_limit_bytes=5 << 20)
    flops = 2 * rows * features * columns

    me = lax.axis_index("feat").astype(jnp.int32).reshape(1)
    chunk = features // ranks
    at = [chunk * count for count in FETCHED]

    def piece(i):
        return VMEM((at[i + 1] - at[i], columns), bf16)

    held_0, listed, adapter_rows, rank_rows, place = pl.pallas_call(
        functools.partial(fetch_and_list_kernel, at[0]),
        out_shape=(piece(0), shape((rows + 2,), jnp.int32)) + (shape((rows, width), jnp.int32),) * 3,
        in_specs=spec(SMEM, 3) + spec(ANY),
        out_specs=spec(VMEM) + spec(SMEM) + spec(VMEM, 3),
        scratch_shapes=[SMEM((adapters,), jnp.int32), pltpu.SemaphoreType.DMA],
        compiler_params=params,
        cost_estimate=cost(0, (at[1] - at[0]) * columns * 2),
    )(me, left_there(adapter_index_table), left_there(adapter_rank_sizes), left_there(query_weight))
    own = tokens.reshape(steps * ranks, chunk)
    across = (swap(own, 2), swap(own, 4), swap(own, 12), swap(own, 8))
    across, held_0, listed = lax.optimization_barrier((across, held_0, listed))
    own_y = across[0]
    near = jnp.concatenate(across[:0:-1], axis=0)
    held_1, down_slices = pl.pallas_call(
        functools.partial(fetch_both_kernel, at[1]),
        out_shape=(piece(1), VMEM((rows, depth, width), bf16)),
        in_specs=spec(SMEM) + spec(ANY, 2),
        out_specs=spec(VMEM, 2),
        scratch_shapes=[pltpu.SemaphoreType.DMA, pltpu.SemaphoreType.DMA],
        compiler_params=params,
        cost_estimate=cost(0, (at[2] - at[1]) * columns * 2 + rows * depth * width * 2),
    )(listed, left_there(query_weight), left_there(adapter_down_weight))
    far = swap(near, 2)
    far, held_1, down_slices = lax.optimization_barrier((far, held_1, down_slices))
    parts = (own, near, own_y, far)
    parts = parts + tuple(swap(part, 1) for part in parts)
    order = ((0,), (8, 12, 4), (2,), (10, 14, 6))
    order = order + tuple(tuple(i ^ 1 for i in owners) for owners in order)

    hidden, held_2 = pl.pallas_call(
        functools.partial(down_kernel, at[2]),
        out_shape=(shape((rows, width), f32), piece(2)),
        in_specs=spec(SMEM) + spec(VMEM, 2 + len(parts) + 1) + spec(ANY),
        out_specs=spec(VMEM, 2),
        scratch_shapes=[pltpu.SemaphoreType.DMA],
        compiler_params=params,
        cost_estimate=cost(2 * rows * depth * width * rows, 1 << 20),
    )(listed, place, adapter_rows, *parts, held_here(down_slices), left_there(query_weight))

    lhs, base, up_slices = pl.pallas_call(
        functools.partial(first_base_kernel, order),
        out_shape=(
            shape((ranks - FETCHED[1], rows, chunk), bf16),
            shape((rows, columns), f32),
            VMEM((rows, width, columns), bf16),
        ),
        in_specs=spec(SMEM, 2) + spec(VMEM, len(parts) + 1) + spec(ANY),
        out_specs=spec(VMEM, 3),
        scratch_shapes=[
            VMEM((depth // LANES, rows * ranks, LANES), f32),
            pltpu.SemaphoreType.DMA,
        ],
        compiler_params=params,
        cost_estimate=cost(flops // 2, 16 << 20),
    )(me, listed, *parts, held_here(held_0), left_there(adapter_up_weight))

    hidden = hidden + swap(hidden, 1)
    three = (swap(hidden, 2), swap(hidden, 4), swap(hidden, 6))
    three, lhs, base, up_slices = lax.optimization_barrier((three, lhs, base, up_slices))
    hidden = hidden + three[0] + three[1] + three[2]

    base = pl.pallas_call(
        rest_base_kernel,
        out_shape=shape((rows, columns), f32),
        in_specs=spec(VMEM, 4) + spec(ANY),
        out_specs=spec(VMEM)[0],
        scratch_shapes=[
            VMEM((ranks - FETCHED[-1], chunk, columns), bf16),
            pltpu.SemaphoreType.DMA((ranks - FETCHED[-1],)),
        ],
        compiler_params=pltpu.CompilerParams(vmem_limit_bytes=(2 * (ranks - FETCHED[-1]) + 3) << 20),
        cost_estimate=cost(flops // 2, 10 << 20),
    )(lhs, base, held_here(held_1), held_here(held_2), left_there(query_weight))
    last, base = lax.optimization_barrier((swap(hidden, 8), base))
    hidden = hidden + last

    out = pl.pallas_call(
        up_kernel,
        out_shape=shape((ranks, steps, columns), bf16),
        in_specs=spec(SMEM) + spec(VMEM, 5),
        out_specs=spec(VMEM)[0],
        compiler_params=params,
        cost_estimate=cost(2 * rows * width * columns * rows, 1 << 20),
    )(listed, adapter_rows, rank_rows, hidden, base, held_here(up_slices))

    gathered = lax.all_to_all(out, "feat", split_axis=0, concat_axis=0, tiled=True)
    return gathered.transpose(1, 0, 2).reshape(steps, 1, features)


def plain(tokens, query_weight, adapter_down_weight, adapter_up_weight, adapter_index_table, adapter_rank_sizes):
    width = query_weight.shape[1]
    rank_width = adapter_down_weight.shape[2]
    depth = adapter_down_weight.shape[1]
    whole = lax.all_gather(tokens, "feat", axis=1, tiled=True)
    piece = lax.dynamic_slice_in_dim(whole, lax.axis_index("feat") * depth, depth, 2)
    matrices = adapter_down_weight[adapter_index_table]
    partial = jnp.einsum("xun,xune->xue", piece, matrices, preferred_element_type=jnp.float32)
    hidden = lax.psum(partial, "feat")
    rank_rows = adapter_rank_sizes[adapter_index_table]
    keep = jnp.arange(rank_width)[None, None, :] < rank_rows[:, :, None]
    factor = 0.25 * rank_width / rank_rows.astype(jnp.float32)
    lowrank = jnp.where(keep, hidden * factor[:, :, None], jnp.float32(0.0)).astype(jnp.bfloat16)
    matrices = adapter_up_weight[adapter_index_table]
    update = jnp.einsum("jma,jmap->jmp", lowrank, matrices, preferred_element_type=jnp.float32)
    base = jnp.einsum("sbd,dc->sbc", whole, query_weight, preferred_element_type=jnp.float32)
    out = (base + update).astype(jnp.bfloat16)
    return lax.all_to_all(out, "feat", split_axis=1, concat_axis=2, tiled=True)


def on_device(tokens, query_weight, *rest):
    ranks = rest[2].shape[1]
    fits = ranks == 16 and query_weight.shape[1] % 256 == 0
    return (fast if fits else plain)(tokens, query_weight, *rest)


def solution(mesh):
    in_specs = (
        P(None, ("rep", "feat"), None),
        P(None, "feat"),
        P(None, "feat", None),
        P(None, None, "feat"),
        P(None, "rep"),
        P(),
    )
    out_specs = P(None, ("rep", "feat"), None)
    return jax.shard_map(
        on_device, mesh=mesh, in_specs=in_specs, out_specs=out_specs, check_vma=False
    )
```

```python
import functools

import jax
import jax.numpy as jnp
from jax import lax
from jax.experimental import pallas as pl
from jax.experimental.pallas import tpu as pltpu
from jax.sharding import PartitionSpec as P

VMEM, SMEM, ANY = pltpu.VMEM, pltpu.SMEM, pl.ANY
GROUP = 8
FETCHED = (0, 7, 10, 13)
LANES = 128


def list_adapters(me, table_ref, sizes_ref, seen, listed, adapter_rows, rank_rows, place):
    steps, owners = table_ref.shape
    rows, lanes = adapter_rows.shape
    for i in range(seen.shape[0]):
        seen[i] = jnp.int32(0)
    for i in range(listed.shape[0]):
        listed[i] = jnp.int32(-1)
    count = jnp.int32(0)
    for b in range(rows):
        adapter = table_ref[b % steps, b // steps]
        new = jnp.int32(1) - seen[adapter]
        seen[adapter] = jnp.int32(1)
        listed[count] = adapter
        count = count + new
        distance = jnp.bitwise_xor(me, jnp.int32(b // steps))
        part = (distance & 1) * 2 + ((distance >> 1) & 1)
        across = (distance >> 2) + jnp.where(distance < 4, 0, jnp.where(distance < 8, 2, -1))
        spot = (part * (owners // 4) + across) * rows + (b % steps) * owners + me
        adapter_rows[b : b + 1, :] = jnp.full((1, lanes), adapter, jnp.int32)
        rank_rows[b : b + 1, :] = jnp.full((1, lanes), sizes_ref[adapter], jnp.int32)
        place[b : b + 1, :] = jnp.full((1, lanes), spot, jnp.int32)
    listed[count] = jnp.int32(-1)
    listed[rows + 1] = count


def padded(count):
    return (count + GROUP - 1) // GROUP * GROUP


def start_slices(listed, weight_ref, held, sem):
    def one(slot, carry):
        adapter = jnp.maximum(listed[slot], 0)
        pltpu.make_async_copy(weight_ref.at[adapter], held.at[slot], sem).start()
        return carry

    lax.fori_loop(0, padded(listed[held.shape[0] + 1]), one, 0)


def wait_slices(listed, weight_ref, held, sem):
    def one(slot, carry):
        pltpu.make_async_copy(weight_ref.at[0], held.at[slot], sem).wait()
        return carry

    lax.fori_loop(0, padded(listed[held.shape[0] + 1]), one, 0)


def fetch_rows(first, weight_ref, held, sem):
    return pltpu.make_async_copy(weight_ref.at[pl.ds(first, held.shape[0])], held, sem)


def fetch_and_list_kernel(
    first, me_ref, table_ref, sizes_ref, weight_ref, held, listed, adapter_rows, rank_rows, place, seen, sem
):
    copy = fetch_rows(first, weight_ref, held, sem)
    copy.start()
    list_adapters(me_ref[0], table_ref, sizes_ref, seen, listed, adapter_rows, rank_rows, place)
    copy.wait()


def fetch_both_kernel(first, listed, weight_ref, slices_ref, held, slices, sem, slice_sem):
    start_slices(listed, slices_ref, slices, slice_sem)
    copy = fetch_rows(first, weight_ref, held, sem)
    copy.start()
    wait_slices(listed, slices_ref, slices, slice_sem)
    copy.wait()


def down_kernel(first_row, listed, place_ref, adapter_rows_ref, *refs):
    *parts, slices, weight_ref, out_ref, held, sem = refs
    copy = fetch_rows(first_row, weight_ref, held, sem)
    copy.start()
    rows, width = out_ref.shape
    place = place_ref[...][:, :1]
    mine = jnp.zeros((rows, slices.shape[1]), jnp.float32)
    first = 0
    for part in parts:
        chosen = lax.broadcasted_iota(jnp.int32, (rows, part.shape[0]), 1) + first == place
        chosen = jnp.where(chosen, jnp.float32(1.0), jnp.float32(0.0)).astype(jnp.bfloat16)
        mine += jnp.dot(chosen, part[...], preferred_element_type=jnp.float32)
        first += part.shape[0]
    mine = mine.astype(jnp.bfloat16)
    adapter_rows = adapter_rows_ref[...]

    def one(group, total):
        for pair in range(0, GROUP, 2):
            slot = group * GROUP + pair
            both = jnp.concatenate([slices[slot], slices[slot + 1]], axis=1)
            product = jnp.dot(mine, both, preferred_element_type=jnp.float32)
            total = jnp.where(adapter_rows == listed[slot], product[:, :width], total)
            total = jnp.where(adapter_rows == listed[slot + 1], product[:, width:], total)
        return total

    zeros = jnp.zeros((rows, width), jnp.float32)
    out_ref[...] = lax.fori_loop(0, padded(listed[rows + 1]) // GROUP, one, zeros)
    copy.wait()


def first_base_kernel(order, me_ref, listed, *refs):
    parts = refs[: len(order)]
    weight, slices_ref, lhs_ref, out_ref, slices, wide, slice_sem = refs[len(order) :]
    start_slices(listed, slices_ref, slices, slice_sem)
    rest, rows, depth = lhs_ref.shape
    chunks = rest + weight.shape[0] // depth
    block = rows // chunks * chunks
    me = me_ref[0]
    for part, owners in zip(parts, order, strict=True):
        for place, distance in enumerate(owners):
            owner = jnp.bitwise_xor(me, distance)
            at = pl.ds(pl.multiple_of(owner * block, block), block)
            for tile in range(depth // LANES):
                piece = part[place * block : (place + 1) * block, tile * LANES : (tile + 1) * LANES]
                wide[tile, at, :] = piece.astype(jnp.float32)

    def whole(chunk):
        pieces = [wide[tile, pl.ds(chunk, rows, stride=chunks), :] for tile in range(depth // LANES)]
        return jnp.concatenate(pieces, axis=1).astype(jnp.bfloat16)

    total = jnp.zeros(out_ref.shape, jnp.float32)
    here = weight.shape[0] // depth
    for chunk in range(here):
        matrix = weight[chunk * depth : (chunk + 1) * depth, :]
        total += jnp.dot(whole(chunk), matrix, preferred_element_type=jnp.float32)
        for other in range(here + chunk, chunks, here):
            lhs_ref[other - here] = whole(other)
    out_ref[...] = total
    wait_slices(listed, slices_ref, slices, slice_sem)


def rest_base_kernel(lhs_ref, base_ref, *refs):
    *weights, rest_ref, out_ref, rest, sems = refs
    chunks, rows, depth = lhs_ref.shape
    streamed = rest.shape[0]
    start = rest_ref.shape[0] - streamed * depth
    copies = []
    for i in range(streamed):
        there = rest_ref.at[pl.ds(start + i * depth, depth)]
        copies.append(pltpu.make_async_copy(there, rest.at[i], sems.at[i]))
        copies[i].start()
    total = base_ref[...]
    chunk = 0
    for weight in weights:
        for first in range(0, weight.shape[0], depth):
            matrix = weight[first : first + depth, :]
            total += jnp.dot(lhs_ref[chunk], matrix, preferred_element_type=jnp.float32)
            chunk += 1
    for i in range(streamed):
        copies[i].wait()
        total += jnp.dot(lhs_ref[chunk + i], rest[i], preferred_element_type=jnp.float32)
    out_ref[...] = total


def up_kernel(listed, adapter_rows_ref, rank_rows_ref, hidden_ref, base_ref, slices, out_ref):
    rows, width = hidden_ref.shape
    rank_rows = rank_rows_ref[...]
    keep = lax.broadcasted_iota(jnp.int32, rank_rows.shape, 1) < rank_rows
    factor = 0.25 * width / rank_rows.astype(jnp.float32)
    lowrank = jnp.where(keep, hidden_ref[...] * factor, jnp.float32(0.0))
    adapter_rows = adapter_rows_ref[...]

    def one(group, total):
        slot = group * GROUP
        own = [jnp.where(adapter_rows == listed[slot + i], lowrank, jnp.float32(0.0)) for i in range(GROUP)]
        own = jnp.concatenate(own, axis=1).astype(jnp.bfloat16)
        matrix = jnp.concatenate([slices[slot + i] for i in range(GROUP)], axis=0)
        return total + jnp.dot(own, matrix, preferred_element_type=jnp.float32)

    total = lax.fori_loop(0, padded(listed[rows + 1]) // GROUP, one, base_ref[...])
    total = total.astype(jnp.bfloat16)
    steps = out_ref.shape[1]
    for owner in range(out_ref.shape[0]):
        out_ref[owner] = total[owner * steps : (owner + 1) * steps, :]


def exchange(value, distance, ranks):
    return lax.ppermute(value, "feat", [(i, i ^ distance) for i in range(ranks)])


def spec(space, count=1):
    return [pl.BlockSpec(memory_space=space)] * count


def cost(flops, size):
    return pl.CostEstimate(flops=flops, bytes_accessed=size, transcendentals=0)


def held_here(value):
    return pltpu.with_memory_space_constraint(value, VMEM)


def left_there(value):
    return pltpu.with_memory_space_constraint(value, pltpu.HBM)


def fast(tokens, query_weight, adapter_down_weight, adapter_up_weight, adapter_index_table, adapter_rank_sizes):
    steps, _, features = tokens.shape
    ranks = adapter_index_table.shape[1]
    columns = query_weight.shape[1]
    adapters, depth, width = adapter_down_weight.shape
    rows = steps * ranks
    bf16, f32 = jnp.bfloat16, jnp.float32
    swap = functools.partial(exchange, ranks=ranks)
    shape = jax.ShapeDtypeStruct
    params = pltpu.CompilerParams(vmem_limit_bytes=5 << 20)
    flops = 2 * rows * features * columns

    me = lax.axis_index("feat").astype(jnp.int32).reshape(1)
    chunk = features // ranks
    at = [chunk * count for count in FETCHED]

    def piece(i):
        return VMEM((at[i + 1] - at[i], columns), bf16)

    held_0, listed, adapter_rows, rank_rows, place = pl.pallas_call(
        functools.partial(fetch_and_list_kernel, at[0]),
        out_shape=(piece(0), shape((rows + 2,), jnp.int32)) + (shape((rows, width), jnp.int32),) * 3,
        in_specs=spec(SMEM, 3) + spec(ANY),
        out_specs=spec(VMEM) + spec(SMEM) + spec(VMEM, 3),
        scratch_shapes=[SMEM((adapters,), jnp.int32), pltpu.SemaphoreType.DMA],
        compiler_params=params,
        cost_estimate=cost(0, (at[1] - at[0]) * columns * 2),
    )(me, left_there(adapter_index_table), left_there(adapter_rank_sizes), left_there(query_weight))
    own = tokens.reshape(steps * ranks, chunk)
    across = (swap(own, 2), swap(own, 4), swap(own, 12), swap(own, 8))
    across, held_0, listed = lax.optimization_barrier((across, held_0, listed))
    own_y = across[0]
    near = jnp.concatenate(across[:0:-1], axis=0)
    held_1, down_slices = pl.pallas_call(
        functools.partial(fetch_both_kernel, at[1]),
        out_shape=(piece(1), VMEM((rows, depth, width), bf16)),
        in_specs=spec(SMEM) + spec(ANY, 2),
        out_specs=spec(VMEM, 2),
        scratch_shapes=[pltpu.SemaphoreType.DMA, pltpu.SemaphoreType.DMA],
        compiler_params=params,
        cost_estimate=cost(0, (at[2] - at[1]) * columns * 2 + rows * depth * width * 2),
    )(listed, left_there(query_weight), left_there(adapter_down_weight))
    far = swap(near, 2)
    far, held_1, down_slices = lax.optimization_barrier((far, held_1, down_slices))
    parts = (own, near, own_y, far)
    parts = parts + tuple(swap(part, 1) for part in parts)
    order = ((0,), (8, 12, 4), (2,), (10, 14, 6))
    order = order + tuple(tuple(i ^ 1 for i in owners) for owners in order)

    hidden, held_2 = pl.pallas_call(
        functools.partial(down_kernel, at[2]),
        out_shape=(shape((rows, width), f32), piece(2)),
        in_specs=spec(SMEM) + spec(VMEM, 2 + len(parts) + 1) + spec(ANY),
        out_specs=spec(VMEM, 2),
        scratch_shapes=[pltpu.SemaphoreType.DMA],
        compiler_params=params,
        cost_estimate=cost(2 * rows * depth * width * rows, 1 << 20),
    )(listed, place, adapter_rows, *parts, held_here(down_slices), left_there(query_weight))

    lhs, base, up_slices = pl.pallas_call(
        functools.partial(first_base_kernel, order),
        out_shape=(
            shape((ranks - FETCHED[1], rows, chunk), bf16),
            shape((rows, columns), f32),
            VMEM((rows, width, columns), bf16),
        ),
        in_specs=spec(SMEM, 2) + spec(VMEM, len(parts) + 1) + spec(ANY),
        out_specs=spec(VMEM, 3),
        scratch_shapes=[
            VMEM((depth // LANES, rows * ranks, LANES), f32),
            pltpu.SemaphoreType.DMA,
        ],
        compiler_params=params,
        cost_estimate=cost(flops // 2, 16 << 20),
    )(me, listed, *parts, held_here(held_0), left_there(adapter_up_weight))

    hidden = hidden + swap(hidden, 1)
    three = (swap(hidden, 2), swap(hidden, 4), swap(hidden, 6))
    three, lhs, base, up_slices = lax.optimization_barrier((three, lhs, base, up_slices))
    hidden = hidden + three[0] + three[1] + three[2]

    base = pl.pallas_call(
        rest_base_kernel,
        out_shape=shape((rows, columns), f32),
        in_specs=spec(VMEM, 4) + spec(ANY),
        out_specs=spec(VMEM)[0],
        scratch_shapes=[
            VMEM((ranks - FETCHED[-1], chunk, columns), bf16),
            pltpu.SemaphoreType.DMA((ranks - FETCHED[-1],)),
        ],
        compiler_params=pltpu.CompilerParams(vmem_limit_bytes=(2 * (ranks - FETCHED[-1]) + 3) << 20),
        cost_estimate=cost(flops // 2, 10 << 20),
    )(lhs, base, held_here(held_1), held_here(held_2), left_there(query_weight))
    last, base = lax.optimization_barrier((swap(hidden, 8), base))
    hidden = hidden + last

    out = pl.pallas_call(
        up_kernel,
        out_shape=shape((ranks, steps, columns), bf16),
        in_specs=spec(SMEM) + spec(VMEM, 5),
        out_specs=spec(VMEM)[0],
        compiler_params=params,
        cost_estimate=cost(2 * rows * width * columns * rows, 1 << 20),
    )(listed, adapter_rows, rank_rows, hidden, base, held_here(up_slices))

    gathered = lax.all_to_all(out, "feat", split_axis=0, concat_axis=0, tiled=True)
    return gathered.transpose(1, 0, 2).reshape(steps, 1, features)


def plain(tokens, query_weight, adapter_down_weight, adapter_up_weight, adapter_index_table, adapter_rank_sizes):
    width = query_weight.shape[1]
    rank_width = adapter_down_weight.shape[2]
    depth = adapter_down_weight.shape[1]
    whole = lax.all_gather(tokens, "feat", axis=1, tiled=True)
    piece = lax.dynamic_slice_in_dim(whole, lax.axis_index("feat") * depth, depth, 2)
    matrices = adapter_down_weight[adapter_index_table]
    partial = jnp.einsum("xun,xune->xue", piece, matrices, preferred_element_type=jnp.float32)
    hidden = lax.psum(partial, "feat")
    rank_rows = adapter_rank_sizes[adapter_index_table]
    keep = jnp.arange(rank_width)[None, None, :] < rank_rows[:, :, None]
    factor = 0.25 * rank_width / rank_rows.astype(jnp.float32)
    lowrank = jnp.where(keep, hidden * factor[:, :, None], jnp.float32(0.0)).astype(jnp.bfloat16)
    matrices = adapter_up_weight[adapter_index_table]
    update = jnp.einsum("jma,jmap->jmp", lowrank, matrices, preferred_element_type=jnp.float32)
    base = jnp.einsum("sbd,dc->sbc", whole, query_weight, preferred_element_type=jnp.float32)
    out = (base + update).astype(jnp.bfloat16)
    return lax.all_to_all(out, "feat", split_axis=1, concat_axis=2, tiled=True)


def on_device(tokens, query_weight, *rest):
    ranks = rest[2].shape[1]
    fits = ranks == 16 and query_weight.shape[1] % 256 == 0
    return (fast if fits else plain)(tokens, query_weight, *rest)


def solution(mesh):
    in_specs = (
        P(None, ("rep", "feat"), None),
        P(None, "feat"),
        P(None, "feat", None),
        P(None, None, "feat"),
        P(None, "rep"),
        P(),
    )
    out_specs = P(None, ("rep", "feat"), None)
    return jax.shard_map(
        on_device, mesh=mesh, in_specs=in_specs, out_specs=out_specs, check_vma=False
    )
```

```python
import functools

import jax
import jax.numpy as jnp
from jax import lax
from jax.experimental import pallas as pl
from jax.experimental.pallas import tpu as pltpu
from jax.sharding import PartitionSpec as P

VMEM, SMEM, ANY = pltpu.VMEM, pltpu.SMEM, pl.ANY
GROUP = 8
FETCHED = (0, 7, 10, 13)
LANES = 128


def list_adapters(me, table_ref, sizes_ref, seen, listed, adapter_rows, rank_rows, place):
    steps, owners = table_ref.shape
    rows, lanes = adapter_rows.shape
    for i in range(seen.shape[0]):
        seen[i] = jnp.int32(0)
    for i in range(listed.shape[0]):
        listed[i] = jnp.int32(-1)
    count = jnp.int32(0)
    for b in range(rows):
        adapter = table_ref[b % steps, b // steps]
        new = jnp.int32(1) - seen[adapter]
        seen[adapter] = jnp.int32(1)
        listed[count] = adapter
        count = count + new
        distance = jnp.bitwise_xor(me, jnp.int32(b // steps))
        part = (distance & 1) * 2 + ((distance >> 1) & 1)
        spot = (part * (owners // 4) + (distance >> 2)) * rows + (b % steps) * owners + me
        adapter_rows[b : b + 1, :] = jnp.full((1, lanes), adapter, jnp.int32)
        rank_rows[b : b + 1, :] = jnp.full((1, lanes), sizes_ref[adapter], jnp.int32)
        place[b : b + 1, :] = jnp.full((1, lanes), spot, jnp.int32)
    listed[count] = jnp.int32(-1)
    listed[rows + 1] = count


def padded(count):
    return (count + GROUP - 1) // GROUP * GROUP


def start_slices(listed, weight_ref, held, sem):
    def one(slot, carry):
        adapter = jnp.maximum(listed[slot], 0)
        pltpu.make_async_copy(weight_ref.at[adapter], held.at[slot], sem).start()
        return carry

    lax.fori_loop(0, padded(listed[held.shape[0] + 1]), one, 0)


def wait_slices(listed, weight_ref, held, sem):
    def one(slot, carry):
        pltpu.make_async_copy(weight_ref.at[0], held.at[slot], sem).wait()
        return carry

    lax.fori_loop(0, padded(listed[held.shape[0] + 1]), one, 0)


def fetch_rows(first, weight_ref, held, sem):
    return pltpu.make_async_copy(weight_ref.at[pl.ds(first, held.shape[0])], held, sem)


def fetch_and_list_kernel(
    first, me_ref, table_ref, sizes_ref, weight_ref, held, listed, adapter_rows, rank_rows, place, seen, sem
):
    copy = fetch_rows(first, weight_ref, held, sem)
    copy.start()
    list_adapters(me_ref[0], table_ref, sizes_ref, seen, listed, adapter_rows, rank_rows, place)
    copy.wait()


def fetch_both_kernel(first, listed, weight_ref, slices_ref, held, slices, sem, slice_sem):
    start_slices(listed, slices_ref, slices, slice_sem)
    copy = fetch_rows(first, weight_ref, held, sem)
    copy.start()
    wait_slices(listed, slices_ref, slices, slice_sem)
    copy.wait()


def down_kernel(first_row, listed, place_ref, adapter_rows_ref, *refs):
    *parts, slices, weight_ref, out_ref, held, sem = refs
    copy = fetch_rows(first_row, weight_ref, held, sem)
    copy.start()
    rows, width = out_ref.shape
    place = place_ref[...][:, :1]
    mine = jnp.zeros((rows, slices.shape[1]), jnp.float32)
    first = 0
    for part in parts:
        chosen = lax.broadcasted_iota(jnp.int32, (rows, part.shape[0]), 1) + first == place
        chosen = jnp.where(chosen, jnp.float32(1.0), jnp.float32(0.0)).astype(jnp.bfloat16)
        mine += jnp.dot(chosen, part[...], preferred_element_type=jnp.float32)
        first += part.shape[0]
    mine = mine.astype(jnp.bfloat16)
    adapter_rows = adapter_rows_ref[...]

    def one(group, total):
        for pair in range(0, GROUP, 2):
            slot = group * GROUP + pair
            both = jnp.concatenate([slices[slot], slices[slot + 1]], axis=1)
            product = jnp.dot(mine, both, preferred_element_type=jnp.float32)
            total = jnp.where(adapter_rows == listed[slot], product[:, :width], total)
            total = jnp.where(adapter_rows == listed[slot + 1], product[:, width:], total)
        return total

    zeros = jnp.zeros((rows, width), jnp.float32)
    out_ref[...] = lax.fori_loop(0, padded(listed[rows + 1]) // GROUP, one, zeros)
    copy.wait()


def first_base_kernel(order, me_ref, listed, *refs):
    parts = refs[: len(order)]
    weight, slices_ref, lhs_ref, out_ref, slices, wide, slice_sem = refs[len(order) :]
    start_slices(listed, slices_ref, slices, slice_sem)
    rest, rows, depth = lhs_ref.shape
    chunks = rest + weight.shape[0] // depth
    block = rows // chunks * chunks
    me = me_ref[0]
    for part, owners in zip(parts, order, strict=True):
        for place, distance in enumerate(owners):
            owner = jnp.bitwise_xor(me, distance)
            at = pl.ds(pl.multiple_of(owner * block, block), block)
            for tile in range(depth // LANES):
                piece = part[place * block : (place + 1) * block, tile * LANES : (tile + 1) * LANES]
                wide[tile, at, :] = piece.astype(jnp.float32)

    def whole(chunk):
        pieces = [wide[tile, pl.ds(chunk, rows, stride=chunks), :] for tile in range(depth // LANES)]
        return jnp.concatenate(pieces, axis=1).astype(jnp.bfloat16)

    total = jnp.zeros(out_ref.shape, jnp.float32)
    here = weight.shape[0] // depth
    for chunk in range(here):
        matrix = weight[chunk * depth : (chunk + 1) * depth, :]
        total += jnp.dot(whole(chunk), matrix, preferred_element_type=jnp.float32)
        for other in range(here + chunk, chunks, here):
            lhs_ref[other - here] = whole(other)
    out_ref[...] = total
    wait_slices(listed, slices_ref, slices, slice_sem)


def rest_base_kernel(lhs_ref, base_ref, *refs):
    *weights, rest_ref, out_ref, rest, sems = refs
    chunks, rows, depth = lhs_ref.shape
    streamed = rest.shape[0]
    start = rest_ref.shape[0] - streamed * depth
    copies = []
    for i in range(streamed):
        there = rest_ref.at[pl.ds(start + i * depth, depth)]
        copies.append(pltpu.make_async_copy(there, rest.at[i], sems.at[i]))
        copies[i].start()
    total = base_ref[...]
    chunk = 0
    for weight in weights:
        for first in range(0, weight.shape[0], depth):
            matrix = weight[first : first + depth, :]
            total += jnp.dot(lhs_ref[chunk], matrix, preferred_element_type=jnp.float32)
            chunk += 1
    for i in range(streamed):
        copies[i].wait()
        total += jnp.dot(lhs_ref[chunk + i], rest[i], preferred_element_type=jnp.float32)
    out_ref[...] = total


def up_kernel(listed, adapter_rows_ref, rank_rows_ref, hidden_ref, base_ref, slices, out_ref):
    rows, width = hidden_ref.shape
    rank_rows = rank_rows_ref[...]
    keep = lax.broadcasted_iota(jnp.int32, rank_rows.shape, 1) < rank_rows
    factor = 0.25 * width / rank_rows.astype(jnp.float32)
    lowrank = jnp.where(keep, hidden_ref[...] * factor, jnp.float32(0.0))
    adapter_rows = adapter_rows_ref[...]

    def one(group, total):
        slot = group * GROUP
        own = [jnp.where(adapter_rows == listed[slot + i], lowrank, jnp.float32(0.0)) for i in range(GROUP)]
        own = jnp.concatenate(own, axis=1).astype(jnp.bfloat16)
        matrix = jnp.concatenate([slices[slot + i] for i in range(GROUP)], axis=0)
        return total + jnp.dot(own, matrix, preferred_element_type=jnp.float32)

    total = lax.fori_loop(0, padded(listed[rows + 1]) // GROUP, one, base_ref[...])
    total = total.astype(jnp.bfloat16)
    steps = out_ref.shape[1]
    for owner in range(out_ref.shape[0]):
        out_ref[owner] = total[owner * steps : (owner + 1) * steps, :]


def exchange(value, distance, ranks):
    return lax.ppermute(value, "feat", [(i, i ^ distance) for i in range(ranks)])


def spec(space, count=1):
    return [pl.BlockSpec(memory_space=space)] * count


def cost(flops, size):
    return pl.CostEstimate(flops=flops, bytes_accessed=size, transcendentals=0)


def held_here(value):
    return pltpu.with_memory_space_constraint(value, VMEM)


def left_there(value):
    return pltpu.with_memory_space_constraint(value, pltpu.HBM)


def fast(tokens, query_weight, adapter_down_weight, adapter_up_weight, adapter_index_table, adapter_rank_sizes):
    steps, _, features = tokens.shape
    ranks = adapter_index_table.shape[1]
    columns = query_weight.shape[1]
    adapters, depth, width = adapter_down_weight.shape
    rows = steps * ranks
    bf16, f32 = jnp.bfloat16, jnp.float32
    swap = functools.partial(exchange, ranks=ranks)
    shape = jax.ShapeDtypeStruct
    params = pltpu.CompilerParams(vmem_limit_bytes=5 << 20)
    flops = 2 * rows * features * columns

    me = lax.axis_index("feat").astype(jnp.int32).reshape(1)
    chunk = features // ranks
    at = [chunk * count for count in FETCHED]

    def piece(i):
        return VMEM((at[i + 1] - at[i], columns), bf16)

    order = ((0, 4, 8, 12, 2), (6, 10, 14))
    order = order + tuple(tuple(i ^ 1 for i in owners) for owners in order)
    held_0, listed, adapter_rows, rank_rows, place = pl.pallas_call(
        functools.partial(fetch_and_list_kernel, at[0]),
        out_shape=(piece(0), shape((rows + 2,), jnp.int32)) + (shape((rows, width), jnp.int32),) * 3,
        in_specs=spec(SMEM, 3) + spec(ANY),
        out_specs=spec(VMEM) + spec(SMEM) + spec(VMEM, 3),
        scratch_shapes=[SMEM((adapters,), jnp.int32), pltpu.SemaphoreType.DMA],
        compiler_params=params,
        cost_estimate=cost(0, (at[1] - at[0]) * columns * 2),
    )(me, left_there(adapter_index_table), left_there(adapter_rank_sizes), left_there(query_weight))
    own = tokens.reshape(steps * ranks, chunk)
    across = (swap(own, 2), swap(own, 4), swap(own, 12), swap(own, 8))
    across, held_0, listed = lax.optimization_barrier((across, held_0, listed))
    own_y = across[0]
    near = jnp.concatenate([across[1], across[3], across[2]], axis=0)
    held_1, down_slices = pl.pallas_call(
        functools.partial(fetch_both_kernel, at[1]),
        out_shape=(piece(1), VMEM((rows, depth, width), bf16)),
        in_specs=spec(SMEM) + spec(ANY, 2),
        out_specs=spec(VMEM, 2),
        scratch_shapes=[pltpu.SemaphoreType.DMA, pltpu.SemaphoreType.DMA],
        compiler_params=params,
        cost_estimate=cost(0, (at[2] - at[1]) * columns * 2 + rows * depth * width * 2),
    )(listed, left_there(query_weight), left_there(adapter_down_weight))
    far = swap(near, 2)
    far, held_1, down_slices = lax.optimization_barrier((far, held_1, down_slices))
    mine = jnp.concatenate([own, near, own_y], axis=0)
    parts = (mine, far, swap(mine, 1), swap(far, 1))

    hidden, held_2 = pl.pallas_call(
        functools.partial(down_kernel, at[2]),
        out_shape=(shape((rows, width), f32), piece(2)),
        in_specs=spec(SMEM) + spec(VMEM, 2 + len(parts) + 1) + spec(ANY),
        out_specs=spec(VMEM, 2),
        scratch_shapes=[pltpu.SemaphoreType.DMA],
        compiler_params=params,
        cost_estimate=cost(2 * rows * depth * width * rows, 1 << 20),
    )(listed, place, adapter_rows, *parts, held_here(down_slices), left_there(query_weight))

    lhs, base, up_slices = pl.pallas_call(
        functools.partial(first_base_kernel, order),
        out_shape=(
            shape((ranks - FETCHED[1], rows, chunk), bf16),
            shape((rows, columns), f32),
            VMEM((rows, width, columns), bf16),
        ),
        in_specs=spec(SMEM, 2) + spec(VMEM, len(parts) + 1) + spec(ANY),
        out_specs=spec(VMEM, 3),
        scratch_shapes=[
            VMEM((depth // LANES, rows * ranks, LANES), f32),
            pltpu.SemaphoreType.DMA,
        ],
        compiler_params=params,
        cost_estimate=cost(flops // 2, 16 << 20),
    )(me, listed, *parts, held_here(held_0), left_there(adapter_up_weight))

    hidden = hidden + swap(hidden, 1)
    three = (swap(hidden, 2), swap(hidden, 4), swap(hidden, 6))
    three, lhs, base, up_slices = lax.optimization_barrier((three, lhs, base, up_slices))
    hidden = hidden + three[0] + three[1] + three[2]

    base = pl.pallas_call(
        rest_base_kernel,
        out_shape=shape((rows, columns), f32),
        in_specs=spec(VMEM, 4) + spec(ANY),
        out_specs=spec(VMEM)[0],
        scratch_shapes=[
            VMEM((ranks - FETCHED[-1], chunk, columns), bf16),
            pltpu.SemaphoreType.DMA((ranks - FETCHED[-1],)),
        ],
        compiler_params=pltpu.CompilerParams(vmem_limit_bytes=(2 * (ranks - FETCHED[-1]) + 3) << 20),
        cost_estimate=cost(flops // 2, 10 << 20),
    )(lhs, base, held_here(held_1), held_here(held_2), left_there(query_weight))
    last, base = lax.optimization_barrier((swap(hidden, 8), base))
    hidden = hidden + last

    out = pl.pallas_call(
        up_kernel,
        out_shape=shape((ranks, steps, columns), bf16),
        in_specs=spec(SMEM) + spec(VMEM, 5),
        out_specs=spec(VMEM)[0],
        compiler_params=params,
        cost_estimate=cost(2 * rows * width * columns * rows, 1 << 20),
    )(listed, adapter_rows, rank_rows, hidden, base, held_here(up_slices))

    gathered = lax.all_to_all(out, "feat", split_axis=0, concat_axis=0, tiled=True)
    return gathered.transpose(1, 0, 2).reshape(steps, 1, features)


def plain(tokens, query_weight, adapter_down_weight, adapter_up_weight, adapter_index_table, adapter_rank_sizes):
    width = query_weight.shape[1]
    rank_width = adapter_down_weight.shape[2]
    depth = adapter_down_weight.shape[1]
    whole = lax.all_gather(tokens, "feat", axis=1, tiled=True)
    piece = lax.dynamic_slice_in_dim(whole, lax.axis_index("feat") * depth, depth, 2)
    matrices = adapter_down_weight[adapter_index_table]
    partial = jnp.einsum("xun,xune->xue", piece, matrices, preferred_element_type=jnp.float32)
    hidden = lax.psum(partial, "feat")
    rank_rows = adapter_rank_sizes[adapter_index_table]
    keep = jnp.arange(rank_width)[None, None, :] < rank_rows[:, :, None]
    factor = 0.25 * rank_width / rank_rows.astype(jnp.float32)
    lowrank = jnp.where(keep, hidden * factor[:, :, None], jnp.float32(0.0)).astype(jnp.bfloat16)
    matrices = adapter_up_weight[adapter_index_table]
    update = jnp.einsum("jma,jmap->jmp", lowrank, matrices, preferred_element_type=jnp.float32)
    base = jnp.einsum("sbd,dc->sbc", whole, query_weight, preferred_element_type=jnp.float32)
    out = (base + update).astype(jnp.bfloat16)
    return lax.all_to_all(out, "feat", split_axis=1, concat_axis=2, tiled=True)


def on_device(tokens, query_weight, *rest):
    ranks = rest[2].shape[1]
    fits = ranks == 16 and query_weight.shape[1] % 256 == 0
    return (fast if fits else plain)(tokens, query_weight, *rest)


def solution(mesh):
    in_specs = (
        P(None, ("rep", "feat"), None),
        P(None, "feat"),
        P(None, "feat", None),
        P(None, None, "feat"),
        P(None, "rep"),
        P(),
    )
    out_specs = P(None, ("rep", "feat"), None)
    return jax.shard_map(
        on_device, mesh=mesh, in_specs=in_specs, out_specs=out_specs, check_vma=False
    )
```

```python
import functools

import jax
import jax.numpy as jnp
from jax import lax
from jax.experimental import pallas as pl
from jax.experimental.pallas import tpu as pltpu
from jax.sharding import PartitionSpec as P

VMEM, SMEM, ANY = pltpu.VMEM, pltpu.SMEM, pl.ANY
GROUP = 8
FETCHED = (0, 7, 10, 13)
LANES = 128


def list_adapters(me, table_ref, sizes_ref, seen, listed, adapter_rows, rank_rows, place):
    steps, owners = table_ref.shape
    rows, lanes = adapter_rows.shape
    for i in range(seen.shape[0]):
        seen[i] = jnp.int32(0)
    for i in range(listed.shape[0]):
        listed[i] = jnp.int32(-1)
    count = jnp.int32(0)
    for b in range(rows):
        adapter = table_ref[b % steps, b // steps]
        new = jnp.int32(1) - seen[adapter]
        seen[adapter] = jnp.int32(1)
        listed[count] = adapter
        count = count + new
        distance = jnp.bitwise_xor(me, jnp.int32(b // steps))
        part = (distance & 1) * 2 + ((distance >> 1) & 1)
        spot = (part * (owners // 4) + (distance >> 2)) * rows + (b % steps) * owners + me
        adapter_rows[b : b + 1, :] = jnp.full((1, lanes), adapter, jnp.int32)
        rank_rows[b : b + 1, :] = jnp.full((1, lanes), sizes_ref[adapter], jnp.int32)
        place[b : b + 1, :] = jnp.full((1, lanes), spot, jnp.int32)
    listed[count] = jnp.int32(-1)
    listed[rows + 1] = count


def padded(count):
    return (count + GROUP - 1) // GROUP * GROUP


def start_slices(listed, weight_ref, held, sem):
    def one(slot, carry):
        adapter = jnp.maximum(listed[slot], 0)
        pltpu.make_async_copy(weight_ref.at[adapter], held.at[slot], sem).start()
        return carry

    lax.fori_loop(0, padded(listed[held.shape[0] + 1]), one, 0)


def wait_slices(listed, weight_ref, held, sem):
    def one(slot, carry):
        pltpu.make_async_copy(weight_ref.at[0], held.at[slot], sem).wait()
        return carry

    lax.fori_loop(0, padded(listed[held.shape[0] + 1]), one, 0)


def fetch_rows(first, weight_ref, held, sem):
    return pltpu.make_async_copy(weight_ref.at[pl.ds(first, held.shape[0])], held, sem)


def fetch_and_list_kernel(
    first, me_ref, table_ref, sizes_ref, weight_ref, held, listed, adapter_rows, rank_rows, place, seen, sem
):
    copy = fetch_rows(first, weight_ref, held, sem)
    copy.start()
    list_adapters(me_ref[0], table_ref, sizes_ref, seen, listed, adapter_rows, rank_rows, place)
    copy.wait()


def fetch_both_kernel(first, listed, weight_ref, slices_ref, held, slices, sem, slice_sem):
    start_slices(listed, slices_ref, slices, slice_sem)
    copy = fetch_rows(first, weight_ref, held, sem)
    copy.start()
    wait_slices(listed, slices_ref, slices, slice_sem)
    copy.wait()


def down_kernel(first_row, listed, place_ref, adapter_rows_ref, *refs):
    *parts, slices, weight_ref, out_ref, held, sem = refs
    copy = fetch_rows(first_row, weight_ref, held, sem)
    copy.start()
    rows, width = out_ref.shape
    place = place_ref[...][:, :1]
    mine = jnp.zeros((rows, slices.shape[1]), jnp.float32)
    first = 0
    for part in parts:
        chosen = lax.broadcasted_iota(jnp.int32, (rows, part.shape[0]), 1) + first == place
        chosen = jnp.where(chosen, jnp.float32(1.0), jnp.float32(0.0)).astype(jnp.bfloat16)
        mine += jnp.dot(chosen, part[...], preferred_element_type=jnp.float32)
        first += part.shape[0]
    mine = mine.astype(jnp.bfloat16)
    adapter_rows = adapter_rows_ref[...]

    def one(group, total):
        for pair in range(0, GROUP, 2):
            slot = group * GROUP + pair
            both = jnp.concatenate([slices[slot], slices[slot + 1]], axis=1)
            product = jnp.dot(mine, both, preferred_element_type=jnp.float32)
            total = jnp.where(adapter_rows == listed[slot], product[:, :width], total)
            total = jnp.where(adapter_rows == listed[slot + 1], product[:, width:], total)
        return total

    zeros = jnp.zeros((rows, width), jnp.float32)
    out_ref[...] = lax.fori_loop(0, padded(listed[rows + 1]) // GROUP, one, zeros)
    copy.wait()


def first_base_kernel(order, me_ref, listed, *refs):
    parts = refs[: len(order)]
    weight, slices_ref, lhs_ref, out_ref, slices, wide, slice_sem = refs[len(order) :]
    start_slices(listed, slices_ref, slices, slice_sem)
    rest, rows, depth = lhs_ref.shape
    chunks = rest + weight.shape[0] // depth
    block = rows // chunks * chunks
    me = me_ref[0]
    for part, owners in zip(parts, order, strict=True):
        for place, distance in enumerate(owners):
            owner = jnp.bitwise_xor(me, distance)
            at = pl.ds(pl.multiple_of(owner * block, block), block)
            for tile in range(depth // LANES):
                piece = part[place * block : (place + 1) * block, tile * LANES : (tile + 1) * LANES]
                wide[tile, at, :] = piece.astype(jnp.float32)

    def whole(chunk):
        pieces = [wide[tile, pl.ds(chunk, rows, stride=chunks), :] for tile in range(depth // LANES)]
        return jnp.concatenate(pieces, axis=1).astype(jnp.bfloat16)

    total = jnp.zeros(out_ref.shape, jnp.float32)
    here = weight.shape[0] // depth
    for chunk in range(here):
        matrix = weight[chunk * depth : (chunk + 1) * depth, :]
        total += jnp.dot(whole(chunk), matrix, preferred_element_type=jnp.float32)
        for other in range(here + chunk, chunks, here):
            lhs_ref[other - here] = whole(other)
    out_ref[...] = total
    wait_slices(listed, slices_ref, slices, slice_sem)


def rest_base_kernel(lhs_ref, base_ref, *refs):
    *weights, rest_ref, out_ref, rest, sems = refs
    chunks, rows, depth = lhs_ref.shape
    streamed = rest.shape[0]
    start = rest_ref.shape[0] - streamed * depth
    copies = []
    for i in range(streamed):
        there = rest_ref.at[pl.ds(start + i * depth, depth)]
        copies.append(pltpu.make_async_copy(there, rest.at[i], sems.at[i]))
        copies[i].start()
    total = base_ref[...]
    chunk = 0
    for weight in weights:
        for first in range(0, weight.shape[0], depth):
            matrix = weight[first : first + depth, :]
            total += jnp.dot(lhs_ref[chunk], matrix, preferred_element_type=jnp.float32)
            chunk += 1
    for i in range(streamed):
        copies[i].wait()
        total += jnp.dot(lhs_ref[chunk + i], rest[i], preferred_element_type=jnp.float32)
    out_ref[...] = total


def up_kernel(listed, adapter_rows_ref, rank_rows_ref, hidden_ref, base_ref, slices, out_ref):
    rows, width = hidden_ref.shape
    rank_rows = rank_rows_ref[...]
    keep = lax.broadcasted_iota(jnp.int32, rank_rows.shape, 1) < rank_rows
    factor = 0.25 * width / rank_rows.astype(jnp.float32)
    lowrank = jnp.where(keep, hidden_ref[...] * factor, jnp.float32(0.0))
    adapter_rows = adapter_rows_ref[...]

    def one(group, total):
        slot = group * GROUP
        own = [jnp.where(adapter_rows == listed[slot + i], lowrank, jnp.float32(0.0)) for i in range(GROUP)]
        own = jnp.concatenate(own, axis=1).astype(jnp.bfloat16)
        matrix = jnp.concatenate([slices[slot + i] for i in range(GROUP)], axis=0)
        return total + jnp.dot(own, matrix, preferred_element_type=jnp.float32)

    total = lax.fori_loop(0, padded(listed[rows + 1]) // GROUP, one, base_ref[...])
    total = total.astype(jnp.bfloat16)
    steps = out_ref.shape[1]
    for owner in range(out_ref.shape[0]):
        out_ref[owner] = total[owner * steps : (owner + 1) * steps, :]


def exchange(value, distance, ranks):
    return lax.ppermute(value, "feat", [(i, i ^ distance) for i in range(ranks)])


def spec(space, count=1):
    return [pl.BlockSpec(memory_space=space)] * count


def cost(flops, size):
    return pl.CostEstimate(flops=flops, bytes_accessed=size, transcendentals=0)


def held_here(value):
    return pltpu.with_memory_space_constraint(value, VMEM)


def left_there(value):
    return pltpu.with_memory_space_constraint(value, pltpu.HBM)


def fast(tokens, query_weight, adapter_down_weight, adapter_up_weight, adapter_index_table, adapter_rank_sizes):
    steps, _, features = tokens.shape
    ranks = adapter_index_table.shape[1]
    columns = query_weight.shape[1]
    adapters, depth, width = adapter_down_weight.shape
    rows = steps * ranks
    bf16, f32 = jnp.bfloat16, jnp.float32
    swap = functools.partial(exchange, ranks=ranks)
    shape = jax.ShapeDtypeStruct
    params = pltpu.CompilerParams(vmem_limit_bytes=5 << 20)
    flops = 2 * rows * features * columns

    me = lax.axis_index("feat").astype(jnp.int32).reshape(1)
    chunk = features // ranks
    at = [chunk * count for count in FETCHED]

    def piece(i):
        return VMEM((at[i + 1] - at[i], columns), bf16)

    order = ((0, 4, 8, 12, 2), (6, 10, 14))
    order = order + tuple(tuple(i ^ 1 for i in owners) for owners in order)
    held_0, listed, adapter_rows, rank_rows, place = pl.pallas_call(
        functools.partial(fetch_and_list_kernel, at[0]),
        out_shape=(piece(0), shape((rows + 2,), jnp.int32)) + (shape((rows, width), jnp.int32),) * 3,
        in_specs=spec(SMEM, 3) + spec(ANY),
        out_specs=spec(VMEM) + spec(SMEM) + spec(VMEM, 3),
        scratch_shapes=[SMEM((adapters,), jnp.int32), pltpu.SemaphoreType.DMA],
        compiler_params=params,
        cost_estimate=cost(0, (at[1] - at[0]) * columns * 2),
    )(me, left_there(adapter_index_table), left_there(adapter_rank_sizes), left_there(query_weight))
    own = tokens.reshape(steps * ranks, chunk)
    across = (swap(own, 2), swap(own, 4), swap(own, 12), swap(own, 8))
    across, held_0, listed = lax.optimization_barrier((across, held_0, listed))
    own_y = across[0]
    near = jnp.concatenate([across[1], across[3], across[2]], axis=0)
    held_1, down_slices = pl.pallas_call(
        functools.partial(fetch_both_kernel, at[1]),
        out_shape=(piece(1), VMEM((rows, depth, width), bf16)),
        in_specs=spec(SMEM) + spec(ANY, 2),
        out_specs=spec(VMEM, 2),
        scratch_shapes=[pltpu.SemaphoreType.DMA, pltpu.SemaphoreType.DMA],
        compiler_params=params,
        cost_estimate=cost(0, (at[2] - at[1]) * columns * 2 + rows * depth * width * 2),
    )(listed, left_there(query_weight), left_there(adapter_down_weight))
    far = swap(near, 2)
    far, held_1, down_slices = lax.optimization_barrier((far, held_1, down_slices))
    mine = jnp.concatenate([own, near, own_y], axis=0)
    parts = (mine, far, swap(mine, 1), swap(far, 1))

    hidden, held_2 = pl.pallas_call(
        functools.partial(down_kernel, at[2]),
        out_shape=(shape((rows, width), f32), piece(2)),
        in_specs=spec(SMEM) + spec(VMEM, 2 + len(parts) + 1) + spec(ANY),
        out_specs=spec(VMEM, 2),
        scratch_shapes=[pltpu.SemaphoreType.DMA],
        compiler_params=params,
        cost_estimate=cost(2 * rows * depth * width * rows, 1 << 20),
    )(listed, place, adapter_rows, *parts, held_here(down_slices), left_there(query_weight))

    lhs, base, up_slices = pl.pallas_call(
        functools.partial(first_base_kernel, order),
        out_shape=(
            shape((ranks - FETCHED[1], rows, chunk), bf16),
            shape((rows, columns), f32),
            VMEM((rows, width, columns), bf16),
        ),
        in_specs=spec(SMEM, 2) + spec(VMEM, len(parts) + 1) + spec(ANY),
        out_specs=spec(VMEM, 3),
        scratch_shapes=[
            VMEM((depth // LANES, rows * ranks, LANES), f32),
            pltpu.SemaphoreType.DMA,
        ],
        compiler_params=params,
        cost_estimate=cost(flops // 2, 16 << 20),
    )(me, listed, *parts, held_here(held_0), left_there(adapter_up_weight))

    hidden = hidden + swap(hidden, 1)
    across = swap(hidden, 8)
    across, lhs, base, up_slices = lax.optimization_barrier((across, lhs, base, up_slices))
    hidden = hidden + across

    base = pl.pallas_call(
        rest_base_kernel,
        out_shape=shape((rows, columns), f32),
        in_specs=spec(VMEM, 4) + spec(ANY),
        out_specs=spec(VMEM)[0],
        scratch_shapes=[
            VMEM((ranks - FETCHED[-1], chunk, columns), bf16),
            pltpu.SemaphoreType.DMA((ranks - FETCHED[-1],)),
        ],
        compiler_params=pltpu.CompilerParams(vmem_limit_bytes=(2 * (ranks - FETCHED[-1]) + 3) << 20),
        cost_estimate=cost(flops // 2, 10 << 20),
    )(lhs, base, held_here(held_1), held_here(held_2), left_there(query_weight))
    near = (swap(hidden, 2), swap(hidden, 4), swap(hidden, 6))
    near, base = lax.optimization_barrier((near, base))
    hidden = hidden + near[0] + near[1] + near[2]

    out = pl.pallas_call(
        up_kernel,
        out_shape=shape((ranks, steps, columns), bf16),
        in_specs=spec(SMEM) + spec(VMEM, 5),
        out_specs=spec(VMEM)[0],
        compiler_params=params,
        cost_estimate=cost(2 * rows * width * columns * rows, 1 << 20),
    )(listed, adapter_rows, rank_rows, hidden, base, held_here(up_slices))

    gathered = lax.all_to_all(out, "feat", split_axis=0, concat_axis=0, tiled=True)
    return gathered.transpose(1, 0, 2).reshape(steps, 1, features)


def plain(tokens, query_weight, adapter_down_weight, adapter_up_weight, adapter_index_table, adapter_rank_sizes):
    width = query_weight.shape[1]
    rank_width = adapter_down_weight.shape[2]
    depth = adapter_down_weight.shape[1]
    whole = lax.all_gather(tokens, "feat", axis=1, tiled=True)
    piece = lax.dynamic_slice_in_dim(whole, lax.axis_index("feat") * depth, depth, 2)
    matrices = adapter_down_weight[adapter_index_table]
    partial = jnp.einsum("xun,xune->xue", piece, matrices, preferred_element_type=jnp.float32)
    hidden = lax.psum(partial, "feat")
    rank_rows = adapter_rank_sizes[adapter_index_table]
    keep = jnp.arange(rank_width)[None, None, :] < rank_rows[:, :, None]
    factor = 0.25 * rank_width / rank_rows.astype(jnp.float32)
    lowrank = jnp.where(keep, hidden * factor[:, :, None], jnp.float32(0.0)).astype(jnp.bfloat16)
    matrices = adapter_up_weight[adapter_index_table]
    update = jnp.einsum("jma,jmap->jmp", lowrank, matrices, preferred_element_type=jnp.float32)
    base = jnp.einsum("sbd,dc->sbc", whole, query_weight, preferred_element_type=jnp.float32)
    out = (base + update).astype(jnp.bfloat16)
    return lax.all_to_all(out, "feat", split_axis=1, concat_axis=2, tiled=True)


def on_device(tokens, query_weight, *rest):
    ranks = rest[2].shape[1]
    fits = ranks == 16 and query_weight.shape[1] % 256 == 0
    return (fast if fits else plain)(tokens, query_weight, *rest)


def solution(mesh):
    in_specs = (
        P(None, ("rep", "feat"), None),
        P(None, "feat"),
        P(None, "feat", None),
        P(None, None, "feat"),
        P(None, "rep"),
        P(),
    )
    out_specs = P(None, ("rep", "feat"), None)
    return jax.shard_map(
        on_device, mesh=mesh, in_specs=in_specs, out_specs=out_specs, check_vma=False
    )
```

```python
import functools

import jax
import jax.numpy as jnp
from jax import lax
from jax.experimental import pallas as pl
from jax.experimental.pallas import tpu as pltpu
from jax.sharding import PartitionSpec as P

VMEM, SMEM, ANY = pltpu.VMEM, pltpu.SMEM, pl.ANY
GROUP = 8
FETCHED = (0, 7, 10, 13)
LANES = 128


def list_adapters(me, table_ref, sizes_ref, seen, listed, adapter_rows, rank_rows, place):
    steps, owners = table_ref.shape
    rows, lanes = adapter_rows.shape
    for i in range(seen.shape[0]):
        seen[i] = jnp.int32(0)
    for i in range(listed.shape[0]):
        listed[i] = jnp.int32(-1)
    count = jnp.int32(0)
    for b in range(rows):
        adapter = table_ref[b % steps, b // steps]
        new = jnp.int32(1) - seen[adapter]
        seen[adapter] = jnp.int32(1)
        listed[count] = adapter
        count = count + new
        distance = jnp.bitwise_xor(me, jnp.int32(b // steps))
        part = (distance & 1) * 2 + ((distance >> 1) & 1)
        spot = (part * (owners // 4) + (distance >> 2)) * rows + (b % steps) * owners + me
        adapter_rows[b : b + 1, :] = jnp.full((1, lanes), adapter, jnp.int32)
        rank_rows[b : b + 1, :] = jnp.full((1, lanes), sizes_ref[adapter], jnp.int32)
        place[b : b + 1, :] = jnp.full((1, lanes), spot, jnp.int32)
    listed[count] = jnp.int32(-1)
    listed[rows + 1] = count


def padded(count):
    return (count + GROUP - 1) // GROUP * GROUP


def start_slices(listed, weight_ref, held, sem):
    def one(slot, carry):
        adapter = jnp.maximum(listed[slot], 0)
        pltpu.make_async_copy(weight_ref.at[adapter], held.at[slot], sem).start()
        return carry

    lax.fori_loop(0, padded(listed[held.shape[0] + 1]), one, 0)


def wait_slices(listed, weight_ref, held, sem):
    def one(slot, carry):
        pltpu.make_async_copy(weight_ref.at[0], held.at[slot], sem).wait()
        return carry

    lax.fori_loop(0, padded(listed[held.shape[0] + 1]), one, 0)


def fetch_rows(first, weight_ref, held, sem):
    return pltpu.make_async_copy(weight_ref.at[pl.ds(first, held.shape[0])], held, sem)


def fetch_and_list_kernel(
    first, me_ref, table_ref, sizes_ref, weight_ref, held, listed, adapter_rows, rank_rows, place, seen, sem
):
    copy = fetch_rows(first, weight_ref, held, sem)
    copy.start()
    list_adapters(me_ref[0], table_ref, sizes_ref, seen, listed, adapter_rows, rank_rows, place)
    copy.wait()


def fetch_both_kernel(first, listed, weight_ref, slices_ref, held, slices, sem, slice_sem):
    start_slices(listed, slices_ref, slices, slice_sem)
    copy = fetch_rows(first, weight_ref, held, sem)
    copy.start()
    wait_slices(listed, slices_ref, slices, slice_sem)
    copy.wait()


def down_kernel(first_row, listed, place_ref, adapter_rows_ref, *refs):
    *parts, slices, weight_ref, out_ref, held, sem = refs
    copy = fetch_rows(first_row, weight_ref, held, sem)
    copy.start()
    rows, width = out_ref.shape
    place = place_ref[...][:, :1]
    mine = jnp.zeros((rows, slices.shape[1]), jnp.float32)
    first = 0
    for part in parts:
        chosen = lax.broadcasted_iota(jnp.int32, (rows, part.shape[0]), 1) + first == place
        chosen = jnp.where(chosen, jnp.float32(1.0), jnp.float32(0.0)).astype(jnp.bfloat16)
        mine += jnp.dot(chosen, part[...], preferred_element_type=jnp.float32)
        first += part.shape[0]
    mine = mine.astype(jnp.bfloat16)
    adapter_rows = adapter_rows_ref[...]

    def one(group, total):
        for pair in range(0, GROUP, 2):
            slot = group * GROUP + pair
            both = jnp.concatenate([slices[slot], slices[slot + 1]], axis=1)
            product = jnp.dot(mine, both, preferred_element_type=jnp.float32)
            total = jnp.where(adapter_rows == listed[slot], product[:, :width], total)
            total = jnp.where(adapter_rows == listed[slot + 1], product[:, width:], total)
        return total

    zeros = jnp.zeros((rows, width), jnp.float32)
    out_ref[...] = lax.fori_loop(0, padded(listed[rows + 1]) // GROUP, one, zeros)
    copy.wait()


def first_base_kernel(order, me_ref, listed, *refs):
    parts = refs[: len(order)]
    weight, slices_ref, lhs_ref, out_ref, slices, wide, slice_sem = refs[len(order) :]
    start_slices(listed, slices_ref, slices, slice_sem)
    rest, rows, depth = lhs_ref.shape
    chunks = rest + weight.shape[0] // depth
    block = rows // chunks * chunks
    me = me_ref[0]
    for part, owners in zip(parts, order, strict=True):
        for place, distance in enumerate(owners):
            owner = jnp.bitwise_xor(me, distance)
            at = pl.ds(pl.multiple_of(owner * block, block), block)
            for tile in range(depth // LANES):
                piece = part[place * block : (place + 1) * block, tile * LANES : (tile + 1) * LANES]
                wide[tile, at, :] = piece.astype(jnp.float32)

    def whole(chunk):
        pieces = [wide[tile, pl.ds(chunk, rows, stride=chunks), :] for tile in range(depth // LANES)]
        return jnp.concatenate(pieces, axis=1).astype(jnp.bfloat16)

    total = jnp.zeros(out_ref.shape, jnp.float32)
    here = weight.shape[0] // depth
    for chunk in range(here):
        matrix = weight[chunk * depth : (chunk + 1) * depth, :]
        total += jnp.dot(whole(chunk), matrix, preferred_element_type=jnp.float32)
        for other in range(here + chunk, chunks, here):
            lhs_ref[other - here] = whole(other)
    out_ref[...] = total
    wait_slices(listed, slices_ref, slices, slice_sem)


def rest_base_kernel(lhs_ref, base_ref, *refs):
    *weights, rest_ref, out_ref, rest, sems = refs
    chunks, rows, depth = lhs_ref.shape
    streamed = rest.shape[0]
    start = rest_ref.shape[0] - streamed * depth
    copies = []
    for i in range(streamed):
        there = rest_ref.at[pl.ds(start + i * depth, depth)]
        copies.append(pltpu.make_async_copy(there, rest.at[i], sems.at[i]))
        copies[i].start()
    total = base_ref[...]
    chunk = 0
    for weight in weights:
        for first in range(0, weight.shape[0], depth):
            matrix = weight[first : first + depth, :]
            total += jnp.dot(lhs_ref[chunk], matrix, preferred_element_type=jnp.float32)
            chunk += 1
    for i in range(streamed):
        copies[i].wait()
        total += jnp.dot(lhs_ref[chunk + i], rest[i], preferred_element_type=jnp.float32)
    out_ref[...] = total


def up_kernel(listed, adapter_rows_ref, rank_rows_ref, hidden_ref, base_ref, slices, out_ref):
    rows, width = hidden_ref.shape
    rank_rows = rank_rows_ref[...]
    keep = lax.broadcasted_iota(jnp.int32, rank_rows.shape, 1) < rank_rows
    factor = 0.25 * width / rank_rows.astype(jnp.float32)
    lowrank = jnp.where(keep, hidden_ref[...] * factor, jnp.float32(0.0))
    adapter_rows = adapter_rows_ref[...]

    def one(group, total):
        slot = group * GROUP
        own = [jnp.where(adapter_rows == listed[slot + i], lowrank, jnp.float32(0.0)) for i in range(GROUP)]
        own = jnp.concatenate(own, axis=1).astype(jnp.bfloat16)
        matrix = jnp.concatenate([slices[slot + i] for i in range(GROUP)], axis=0)
        return total + jnp.dot(own, matrix, preferred_element_type=jnp.float32)

    total = lax.fori_loop(0, padded(listed[rows + 1]) // GROUP, one, base_ref[...])
    total = total.astype(jnp.bfloat16)
    steps = out_ref.shape[1]
    for owner in range(out_ref.shape[0]):
        out_ref[owner] = total[owner * steps : (owner + 1) * steps, :]


def exchange(value, distance, ranks):
    return lax.ppermute(value, "feat", [(i, i ^ distance) for i in range(ranks)])


def spec(space, count=1):
    return [pl.BlockSpec(memory_space=space)] * count


def cost(flops, size):
    return pl.CostEstimate(flops=flops, bytes_accessed=size, transcendentals=0)


def held_here(value):
    return pltpu.with_memory_space_constraint(value, VMEM)


def left_there(value):
    return pltpu.with_memory_space_constraint(value, pltpu.HBM)


def fast(tokens, query_weight, adapter_down_weight, adapter_up_weight, adapter_index_table, adapter_rank_sizes):
    steps, _, features = tokens.shape
    ranks = adapter_index_table.shape[1]
    columns = query_weight.shape[1]
    adapters, depth, width = adapter_down_weight.shape
    rows = steps * ranks
    bf16, f32 = jnp.bfloat16, jnp.float32
    swap = functools.partial(exchange, ranks=ranks)
    shape = jax.ShapeDtypeStruct
    params = pltpu.CompilerParams(vmem_limit_bytes=5 << 20)
    flops = 2 * rows * features * columns

    me = lax.axis_index("feat").astype(jnp.int32).reshape(1)
    chunk = features // ranks
    at = [chunk * count for count in FETCHED]

    def piece(i):
        return VMEM((at[i + 1] - at[i], columns), bf16)

    order = ((0, 4, 8, 12, 2), (6, 10, 14))
    order = order + tuple(tuple(i ^ 1 for i in owners) for owners in order)
    held_0, listed, adapter_rows, rank_rows, place = pl.pallas_call(
        functools.partial(fetch_and_list_kernel, at[0]),
        out_shape=(piece(0), shape((rows + 2,), jnp.int32)) + (shape((rows, width), jnp.int32),) * 3,
        in_specs=spec(SMEM, 3) + spec(ANY),
        out_specs=spec(VMEM) + spec(SMEM) + spec(VMEM, 3),
        scratch_shapes=[SMEM((adapters,), jnp.int32), pltpu.SemaphoreType.DMA],
        compiler_params=params,
        cost_estimate=cost(0, (at[1] - at[0]) * columns * 2),
    )(me, left_there(adapter_index_table), left_there(adapter_rank_sizes), left_there(query_weight))
    own = tokens.reshape(steps * ranks, chunk)
    across = (swap(own, 4), swap(own, 2), swap(own, 12), swap(own, 8))
    across, held_0, listed = lax.optimization_barrier((across, held_0, listed))
    own_y = across[1]
    near = jnp.concatenate([across[0], across[3], across[2]], axis=0)
    held_1, down_slices = pl.pallas_call(
        functools.partial(fetch_both_kernel, at[1]),
        out_shape=(piece(1), VMEM((rows, depth, width), bf16)),
        in_specs=spec(SMEM) + spec(ANY, 2),
        out_specs=spec(VMEM, 2),
        scratch_shapes=[pltpu.SemaphoreType.DMA, pltpu.SemaphoreType.DMA],
        compiler_params=params,
        cost_estimate=cost(0, (at[2] - at[1]) * columns * 2 + rows * depth * width * 2),
    )(listed, left_there(query_weight), left_there(adapter_down_weight))
    far = swap(near, 2)
    far, held_1, down_slices = lax.optimization_barrier((far, held_1, down_slices))
    mine = jnp.concatenate([own, near, own_y], axis=0)
    parts = (mine, far, swap(mine, 1), swap(far, 1))

    hidden, held_2 = pl.pallas_call(
        functools.partial(down_kernel, at[2]),
        out_shape=(shape((rows, width), f32), piece(2)),
        in_specs=spec(SMEM) + spec(VMEM, 2 + len(parts) + 1) + spec(ANY),
        out_specs=spec(VMEM, 2),
        scratch_shapes=[pltpu.SemaphoreType.DMA],
        compiler_params=params,
        cost_estimate=cost(2 * rows * depth * width * rows, 1 << 20),
    )(listed, place, adapter_rows, *parts, held_here(down_slices), left_there(query_weight))

    lhs, base, up_slices = pl.pallas_call(
        functools.partial(first_base_kernel, order),
        out_shape=(
            shape((ranks - FETCHED[1], rows, chunk), bf16),
            shape((rows, columns), f32),
            VMEM((rows, width, columns), bf16),
        ),
        in_specs=spec(SMEM, 2) + spec(VMEM, len(parts) + 1) + spec(ANY),
        out_specs=spec(VMEM, 3),
        scratch_shapes=[
            VMEM((depth // LANES, rows * ranks, LANES), f32),
            pltpu.SemaphoreType.DMA,
        ],
        compiler_params=params,
        cost_estimate=cost(flops // 2, 16 << 20),
    )(me, listed, *parts, held_here(held_0), left_there(adapter_up_weight))

    hidden = hidden + swap(hidden, 1)
    across = swap(hidden, 8)
    across, lhs, base, up_slices = lax.optimization_barrier((across, lhs, base, up_slices))
    hidden = hidden + across

    base = pl.pallas_call(
        rest_base_kernel,
        out_shape=shape((rows, columns), f32),
        in_specs=spec(VMEM, 4) + spec(ANY),
        out_specs=spec(VMEM)[0],
        scratch_shapes=[
            VMEM((ranks - FETCHED[-1], chunk, columns), bf16),
            pltpu.SemaphoreType.DMA((ranks - FETCHED[-1],)),
        ],
        compiler_params=pltpu.CompilerParams(vmem_limit_bytes=(2 * (ranks - FETCHED[-1]) + 3) << 20),
        cost_estimate=cost(flops // 2, 10 << 20),
    )(lhs, base, held_here(held_1), held_here(held_2), left_there(query_weight))
    near = (swap(hidden, 2), swap(hidden, 4), swap(hidden, 6))
    near, base = lax.optimization_barrier((near, base))
    hidden = hidden + near[0] + near[1] + near[2]

    out = pl.pallas_call(
        up_kernel,
        out_shape=shape((ranks, steps, columns), bf16),
        in_specs=spec(SMEM) + spec(VMEM, 5),
        out_specs=spec(VMEM)[0],
        compiler_params=params,
        cost_estimate=cost(2 * rows * width * columns * rows, 1 << 20),
    )(listed, adapter_rows, rank_rows, hidden, base, held_here(up_slices))

    gathered = lax.all_to_all(out, "feat", split_axis=0, concat_axis=0, tiled=True)
    return gathered.transpose(1, 0, 2).reshape(steps, 1, features)


def plain(tokens, query_weight, adapter_down_weight, adapter_up_weight, adapter_index_table, adapter_rank_sizes):
    width = query_weight.shape[1]
    rank_width = adapter_down_weight.shape[2]
    depth = adapter_down_weight.shape[1]
    whole = lax.all_gather(tokens, "feat", axis=1, tiled=True)
    piece = lax.dynamic_slice_in_dim(whole, lax.axis_index("feat") * depth, depth, 2)
    matrices = adapter_down_weight[adapter_index_table]
    partial = jnp.einsum("xun,xune->xue", piece, matrices, preferred_element_type=jnp.float32)
    hidden = lax.psum(partial, "feat")
    rank_rows = adapter_rank_sizes[adapter_index_table]
    keep = jnp.arange(rank_width)[None, None, :] < rank_rows[:, :, None]
    factor = 0.25 * rank_width / rank_rows.astype(jnp.float32)
    lowrank = jnp.where(keep, hidden * factor[:, :, None], jnp.float32(0.0)).astype(jnp.bfloat16)
    matrices = adapter_up_weight[adapter_index_table]
    update = jnp.einsum("jma,jmap->jmp", lowrank, matrices, preferred_element_type=jnp.float32)
    base = jnp.einsum("sbd,dc->sbc", whole, query_weight, preferred_element_type=jnp.float32)
    out = (base + update).astype(jnp.bfloat16)
    return lax.all_to_all(out, "feat", split_axis=1, concat_axis=2, tiled=True)


def on_device(tokens, query_weight, *rest):
    ranks = rest[2].shape[1]
    fits = ranks == 16 and query_weight.shape[1] % 256 == 0
    return (fast if fits else plain)(tokens, query_weight, *rest)


def solution(mesh):
    in_specs = (
        P(None, ("rep", "feat"), None),
        P(None, "feat"),
        P(None, "feat", None),
        P(None, None, "feat"),
        P(None, "rep"),
        P(),
    )
    out_specs = P(None, ("rep", "feat"), None)
    return jax.shard_map(
        on_device, mesh=mesh, in_specs=in_specs, out_specs=out_specs, check_vma=False
    )
```
